128 devices in a mesh: ta: 16 (over z_hi, y, core), sa: 8 (over z_lo, x).
Axes of the slice: x: 4, y: 4, z: 4 (z_hi: 2, z_lo: 2; z = z_hi * 2 + z_lo), core: 2. Of those that a mesh axis runs over, the one named last changes fastest.
Arguments:
- video_q: bfloat16 [16, 8, 256, 3072], P('ta', 'sa'), may hold values from -120 to 120
- video_kv: bfloat16 [16, 8, 256, 6144], P('ta', 'sa'), may hold values from -6 to 6
- text_qkv: bfloat16 [256, 9216], P(('ta', 'sa')), may hold values from -120 to 120
- text_mask: int32 [256], replicated, may hold values 0 or 1
- pattern: int32 [16, 8, 4], P('ta', 'sa'), may hold values from -1 to 127, as said below
Outputs:
- video_out: bfloat16 [16, 8, 256, 3072], P('ta', 'sa')
- text_out: bfloat16 [256, 3072], P(('ta', 'sa'))
The draws below stay inside these ranges and needn't reach their ends.
Inputs may be any that keep to these rules, and one draw needn't show every extreme that they name: `pattern`: for tile (t, s) the row lists distinct indices of the tile itself (always first) and of tiles one step away along time or along space, then -1 in unused slots; it lists 1 to 4 tiles, and in every draw some tiles list 4.
All inputs are finite; a program needn't handle non-finite values.
Results may differ from the reference program's by a relative error of at most 0.03.
Values may be sent and summed in bfloat16 or wider, within the bound.
A program may use at most 768 MiB of HBM per device.

```python
import math
import jax
import jax.numpy as jnp
from jax import lax

HEAD = 128
D = 3072
TEXT = 256
TILE = 256
NB = 4
N_TA = 16
N_SA = 8


def shared_keys(key):
    return jax.random.truncated_normal(key, -6.0, 6.0, (N_TA, N_SA, TILE, 2 * D), jnp.float32)


def draw_video_kv(key, part):
    base_keys = shared_keys(key)
    return base_keys.astype(jnp.bfloat16)


def draw_video_q(key, part):
    key = jax.random.fold_in(key, 5)
    noise_draw = jax.random.truncated_normal(key, -6.0, 6.0, (N_TA, N_SA, TILE, D), jnp.float32)
    return noise_draw.astype(jnp.bfloat16)


def draw_text_qkv(key, part):
    key = jax.random.fold_in(key, 9)
    values = jax.random.truncated_normal(key, -6.0, 6.0, (TEXT, 3 * D), jnp.float32)
    return values.astype(jnp.bfloat16)


def draw_pattern(key, part):
    key = jax.random.fold_in(key, 7)
    key_one, key_two, key_three = jax.random.split(key, 3)
    time_ids = jnp.arange(N_TA, dtype=jnp.int32)[:, None, None]
    space_ids = jnp.arange(N_SA, dtype=jnp.int32)[None, :, None]
    time_moves = jnp.array([0, -1, 1, 0, 0], jnp.int32)
    space_moves = jnp.array([0, 0, 0, -1, 1], jnp.int32)
    near_time = jnp.broadcast_to(time_ids + time_moves, (N_TA, N_SA, 5))
    near_space = jnp.broadcast_to(space_ids + space_moves, (N_TA, N_SA, 5))
    inside = (near_time >= 0) & (near_time < N_TA) & (near_space >= 0) & (near_space < N_SA)
    targets = near_time * N_SA + near_space
    candidate = jnp.arange(5, dtype=jnp.int32)
    scores = jax.random.randint(key_one, (N_TA, N_SA, 5), 0, 1000) * 8 + candidate
    scores = jnp.where(candidate == 0, -1, scores)
    scores = jnp.where(inside, scores, 100000)
    order = jnp.argsort(scores, axis=-1, stable=True)[..., :NB]
    picked = jnp.take_along_axis(targets, order, axis=-1)
    available = jnp.sum(inside.astype(jnp.int32), axis=-1)
    counts = jax.random.randint(key_two, (N_TA, N_SA), 1, NB + 1)
    residue = jax.random.randint(key_three, (), 0, 3)
    tile_ids = time_ids[..., 0] * N_SA + space_ids[..., 0]
    counts = jnp.where(tile_ids % 3 == residue, NB, counts)
    counts = jnp.minimum(counts, available)
    slot_ids = jnp.arange(NB, dtype=jnp.int32)
    return jnp.where(slot_ids < counts[..., None], picked, -1).astype(jnp.int32)


def set_ends(values, rng, low, largest):
    longest = values.shape.index(max(values.shape))
    spots = []
    for shift in (0, 1):
        where = [jax.random.randint(jax.random.fold_in(rng, axis), (), 0, length) for axis, length in enumerate(values.shape)]
        where[longest] = (where[longest] + shift) % values.shape[longest]
        spots.append(tuple(where))
    return values.at[spots[0]].set(low).at[spots[1]].set(largest)


def setup_inputs(seed: int = 0) -> dict:
    splits = jax.random.split(jax.random.key(seed), 6)
    video_q = draw_video_q(jax.random.fold_in(splits[5], 71), 0)
    video_kv = draw_video_kv(jax.random.fold_in(splits[5], 71), 0)
    text_qkv = draw_text_qkv(jax.random.fold_in(splits[5], 71), 0)
    text_mask = set_ends((jax.random.randint(splits[3], (TEXT,), 0, 4) < 3).astype(jnp.int32), jax.random.fold_in(splits[3], 1), 0, 1)
    pattern = draw_pattern(jax.random.fold_in(splits[5], 71), 0)
    return dict(video_q=video_q, video_kv=video_kv, text_qkv=text_qkv, text_mask=text_mask, pattern=pattern)


def attend(query, key_rows, value_rows, is_valid):
    head_count = query.shape[1] // HEAD
    scale = 1.0 / math.sqrt(HEAD)

    def one_head(head_index):
        first_col = head_index * HEAD
        q_part = lax.dynamic_slice_in_dim(query, first_col, HEAD, 1)
        k_part = lax.dynamic_slice_in_dim(key_rows, first_col, HEAD, 1)
        v_part = lax.dynamic_slice_in_dim(value_rows, first_col, HEAD, 1)
        scores = lax.dot_general(q_part, k_part, (((1,), (1,)), ((), ())), preferred_element_type=jnp.float32) * scale
        scores = jnp.where(is_valid[None, :], scores, -1e+30)
        row_top = lax.optimization_barrier(jnp.max(scores, axis=1, keepdims=True))
        weights = jnp.exp(scores - row_top)
        row_total = lax.optimization_barrier(jnp.sum(weights, axis=1, keepdims=True))
        mixed = jnp.dot(weights.astype(jnp.bfloat16), v_part, preferred_element_type=jnp.float32)
        return mixed / row_total
    stacked = lax.map(one_head, jnp.arange(head_count, dtype=jnp.int32))
    return jnp.transpose(stacked, (1, 0, 2)).reshape(query.shape[0], head_count * HEAD).astype(jnp.bfloat16)

def reference(video_q, video_kv, text_qkv, text_mask, pattern):
    tile_count = N_TA * N_SA
    flat_q = video_q.reshape(tile_count, TILE, D)
    flat_kv = video_kv.reshape(tile_count, TILE, 2 * D)
    pattern_rows = pattern.reshape(tile_count, NB)
    text_keys = text_qkv[:, D:2 * D]
    text_values = text_qkv[:, 2 * D:]
    text_valid = text_mask == 1

    def one_tile(tile_index):
        tile_row = pattern_rows[tile_index]
        chosen = jnp.take(flat_kv, jnp.clip(tile_row, 0, tile_count - 1), axis=0).reshape(NB * TILE, 2 * D)
        key_rows = jnp.concatenate([chosen[:, :D], text_keys], axis=0)
        value_rows = jnp.concatenate([chosen[:, D:], text_values], axis=0)
        is_valid = jnp.concatenate([jnp.repeat(tile_row >= 0, TILE), text_valid])
        return attend(flat_q[tile_index], key_rows, value_rows, is_valid)
    video_out = lax.map(one_tile, jnp.arange(tile_count, dtype=jnp.int32)).reshape(N_TA, N_SA, TILE, D)
    all_kv = flat_kv.reshape(tile_count * TILE, 2 * D)
    key_rows = jnp.concatenate([all_kv[:, :D], text_keys], axis=0)
    value_rows = jnp.concatenate([all_kv[:, D:], text_values], axis=0)
    is_valid = jnp.concatenate([jnp.ones((tile_count * TILE,), dtype=bool), text_valid])
    text_out = attend(text_qkv[:, :D], key_rows, value_rows, is_valid)
    return (video_out, text_out)
```

```python
import functools
import math

import jax
import jax.numpy as jnp
from jax import lax
from jax.experimental import pallas as pl
from jax.experimental.pallas import tpu as pltpu
from jax.sharding import PartitionSpec as P

HEAD = 128
D = 3072
TILE = 256
HEADS = 24
HALF = 12
CHUNKS = 12
CW = D // CHUNKS
TCOLS = 3 * D
THALF = TCOLS // 2
TQ = THALF // 2
SEC = TQ // 3
MESH = pl.DeviceIdType.MESH
C2 = math.log2(math.e) / math.sqrt(HEAD)
NEG = -1e30
PAIR, FAR, LEFT, RIGHT, OWN = 0, 1, 2, 3, 4


def qk(q, k):
    return lax.dot_general(q, k, (((1,), (1,)), ((), ())), preferred_element_type=jnp.float32)


def pv(p, v):
    return jnp.dot(p.astype(jnp.bfloat16), v, preferred_element_type=jnp.float32)


def merge(parts, stats, out, out_stats, last):
    top = functools.reduce(jnp.maximum, [m for m, _ in stats])
    weights = [jnp.exp2(m - top) for m, _ in stats]
    total = sum(w * l for w, (_, l) in zip(weights, stats))
    if last:
        weights = [w / total for w in weights]
    else:
        out_stats(top, total)
    for h in range(HALF):
        mixed = sum(
            w[..., h : h + 1] * part(h).astype(jnp.float32) for w, part in zip(weights, parts)
        )
        out(h, mixed.astype(jnp.bfloat16))


def kernel(
    q_hbm, kv_hbm, text_ref, mask_ref, pat_ref, video_ref, tout_ref,
    buf, q, stage, G, T, bias_ref, bias2_ref, Pt, PS, RB1, RS1, P2, S2, RB2, RS2, P3, S3, RB3, RS3, full,
    lsem, g_s, g_r, a_s, a_r, x_s, x_r, pair_s, pair_r, hs, hr, fwd_s, r_s, r_r,
):
    t = lax.axis_index("ta")
    s = lax.axis_index("sa")
    core = lax.rem(t, 2)
    y = lax.rem(t // 2, 4)
    x = lax.rem(s, 4)
    z = (t // 8) * 2 + s // 4
    g = x * 2 + core

    def dev(x_, y_, z_, core_):
        return ((z_ // 2) * 8 + y_ * 2 + core_, lax.rem(z_, 2) * 4 + x_)

    def up(v, i, n=4):
        return lax.rem(v + i, n)

    pair_t = t + 1 - 2 * core
    far_t = t + 2 * core - 1
    has_far = jnp.logical_and(far_t >= 0, far_t <= 15)
    has_left = s > 0
    has_right = s < 7
    far_cross = jnp.logical_or(t == 7, t == 8)
    far_relay = jnp.logical_or(t == 0, t == 15)
    relay_out_t = jnp.where(core == 1, 15, 0)
    relay_fin_t = jnp.where(t == 15, 8, 7)

    def g_peer(i):
        gg = up(g, i, 8)
        return dev(gg // 2, y, z, lax.rem(gg, 2))

    own_copy = pltpu.make_async_copy(kv_hbm, buf.at[OWN], lsem.at[0])
    q_copy = pltpu.make_async_copy(q_hbm, q, lsem.at[1])
    own_copy.start()
    q_copy.start()
    barrier = pltpu.get_barrier_semaphore()

    def greet(device):
        pl.semaphore_signal(barrier, inc=1, device_id=device, device_id_type=MESH)

    for i in range(1, 8):
        greet(g_peer(i))
    for i in range(1, 4):
        greet(dev(x, y, up(z, i), core))
        greet(dev(x, up(y, i), z, core))
    extra = [
        (has_far, (far_t, s)),
        (s == 3, (t, 4)),
        (s == 4, (t, 3)),
        (t == 15, (8, s)),
        (t == 8, (15, s)),
        (t == 0, (7, s)),
        (t == 7, (0, s)),
    ]
    for cond, device in extra:

        @pl.when(cond)
        def _():
            greet(device)

    rows = text_ref[...].astype(jnp.float32)
    w8 = TCOLS // 8
    stage[...] = jnp.concatenate(
        [rows[:, j * w8 : (j + 1) * w8] for j in range(8)], axis=0
    ).astype(jnp.bfloat16)

    pl.semaphore_wait(barrier, 13 + sum(jnp.where(cond, 1, 0) for cond, _ in extra))

    def remote(src, dst, ssem, rsem, device):
        return pltpu.make_async_remote_copy(
            src_ref=src, dst_ref=dst, send_sem=ssem, recv_sem=rsem,
            device_id=device, device_id_type=MESH,
        )

    def g_copy(i, slot):
        return remote(stage, G.at[slot], g_s.at[i], g_r.at[i], g_peer(i))

    for i in range(1, 8):
        g_copy(i, g).start()
    G[pl.ds(g, 1)] = stage[...][None]

    def cols(c, sec):
        return pl.ds(pl.multiple_of(c * CW + sec * D, 128), CW)

    def halo(k, c, sec, src, slot, device):
        return remote(
            src.at[:, cols(c, sec)], buf.at[slot, :, cols(c, sec)],
            hs.at[k], hr.at[slot, c, sec], device,
        )

    def send_halo(k, c):
        odd = lax.rem(c, 2) == 1
        if k == FAR:
            relay = jnp.logical_and(far_cross, odd)
            device = (jnp.where(relay, relay_out_t, far_t), s)
            slot = FAR
        elif k == LEFT:
            relay = jnp.logical_and(s == 4, odd)
            device = (t, jnp.where(relay, 0, s - 1))
            slot = jnp.where(relay, LEFT, RIGHT)
        else:
            relay = jnp.logical_and(s == 3, odd)
            device = (t, jnp.where(relay, 7, s + 1))
            slot = jnp.where(relay, RIGHT, LEFT)
        for sec in range(2):
            halo(k, c, sec, kv_hbm, slot, device).start()

    def send_loop(conds):
        @functools.partial(lax.fori_loop, 0, CHUNKS, init_val=0)
        def _(c, carry):
            for k, cond in conds:

                @pl.when(cond)
                def _():
                    send_halo(k, c)

            return carry

    send_loop([(LEFT, jnp.logical_and(has_left, s != 4)), (RIGHT, jnp.logical_and(has_right, s != 3))])

    def pair_copy():
        return remote(kv_hbm, buf.at[PAIR], pair_s, pair_r, (pair_t, s))

    pair_copy().start()

    for i in range(1, 8):
        g_copy(i, up(g, 8 - i, 8)).wait_recv()
    r_ = lax.broadcasted_iota(jnp.int32, (128, 128), 0)
    c_ = lax.broadcasted_iota(jnp.int32, (128, 128), 1)
    swap = (r_ // 16 == lax.rem(c_, 16) // 2) & (lax.rem(r_, 16) // 2 == c_ // 16)
    swap = swap & (lax.rem(r_, 2) == lax.rem(c_, 2))
    mixed_rows = jnp.dot(
        jnp.where(swap, 1.0, 0.0).astype(jnp.bfloat16),
        G[...].reshape(128, w8),
        preferred_element_type=jnp.float32,
    ).astype(jnp.bfloat16)
    def place(cc):
        for sec in range(3):
            for n in range(4):
                p = (sec * 4 + cc * 2) * 2 + n
                j, off = p // 3, (p % 3) * 384
                col = cc * THALF + (n // 2) * TQ + sec * SEC + (n % 2) * 384
                T[pl.ds(y, 1), pl.ds(z, 1), :, col : col + 384] = mixed_rows[
                    16 * j : 16 * j + 16, off : off + 384
                ][None, None]

    pl.when(core == 0)(lambda: place(0))
    pl.when(core == 1)(lambda: place(1))

    base = core * THALF
    ca = pl.ds(pl.multiple_of(base, 128), TQ)
    cb = pl.ds(pl.multiple_of(base + TQ, 128), TQ)

    def step_copy(step, half, i, yy, zz):
        along_z = (step == 0) == (half == 0)
        cs = ca if half == 0 else cb
        if step == 0:
            ref = T.at[yy, zz, :, cs]
        elif half == 0:
            ref = T.at[yy, :, :, cs]
        else:
            ref = T.at[:, zz, :, cs]
        device = dev(x, y, up(z, i), core) if along_z else dev(x, up(y, i), z, core)
        return remote(ref, ref, a_s.at[step, half, i], a_r.at[step, half, i], device)

    def step_waits(step):
        for half in range(2):
            along_z = (step == 0) == (half == 0)
            for i in range(1, 4):
                if along_z:
                    step_copy(step, half, i, y, up(z, 4 - i)).wait_recv()
                else:
                    step_copy(step, half, i, up(y, 4 - i), z).wait_recv()

    for step in range(2):
        for i in range(1, 4):
            for half in range(2):
                step_copy(step, half, i, y, z).start()
        step_waits(step)

    own_half = T.at[:, :, :, pl.ds(pl.multiple_of(base, 128), THALF)]
    other_half = T.at[:, :, :, pl.ds(pl.multiple_of(THALF - base, 128), THALF)]
    half_out = remote(own_half, own_half, x_s, x_r, (pair_t, s))
    half_in = remote(other_half, other_half, x_s, x_r, (pair_t, s))
    half_out.start()
    send_loop([(LEFT, s == 4), (RIGHT, s == 3)])

    r_ = lax.broadcasted_iota(jnp.int32, (256, 256), 0)
    c_ = lax.broadcasted_iota(jnp.int32, (256, 256), 1)
    by, bz, bx = c_ // 64, lax.rem(c_ // 16, 4), lax.rem(c_, 16) // 4
    bc, bi = lax.rem(c_ // 2, 2), lax.rem(c_, 2)
    row_of = (((bz // 2) * 8 + by * 2 + bc) * 8 + lax.rem(bz, 2) * 4 + bx) * 2 + bi
    valid = jnp.where(mask_ref[...] == 1, 1.0, 0.0)
    hot = jnp.where(r_ == row_of, 1.0, 0.0).astype(jnp.bfloat16)
    kept = jnp.dot(
        jnp.broadcast_to(valid, (8, 256)).astype(jnp.bfloat16), hot,
        preferred_element_type=jnp.float32,
    )
    bias = jnp.where(kept > 0.5, 0.0, NEG)
    bias_ref[...] = bias
    lane = lax.broadcasted_iota(jnp.int32, (8, 256), 1)
    mine = jnp.where(lane // 16 == y * 4 + z, 1, 0) * jnp.where(x == 0, 1, 0)
    bias2_ref[...] = jnp.where(mine == 1, bias, NEG)

    own_copy.wait()
    q_copy.wait()
    pair_copy().wait_recv()
    PS[...] = jnp.zeros_like(PS)

    def hcol(v):
        return pl.ds(pl.multiple_of(v, 128), HEAD)

    def text_cols(col):
        return T[:, :, :, hcol(col)].reshape(256, HEAD)

    @functools.partial(lax.fori_loop, 0, HALF, init_val=0)
    def _(hh, carry):
        col = base + (hh // 6) * TQ + lax.rem(hh, 6) * HEAD
        kcol = core * (D // 2) + hh * HEAD
        qx = text_cols(col)
        parts = [
            (qk(qx, buf[OWN, :, hcol(kcol)]), buf[OWN, :, hcol(kcol + D)]),
            (qk(qx, buf[PAIR, :, hcol(kcol)]), buf[PAIR, :, hcol(kcol + D)]),
            (qk(qx, text_cols(col + SEC)) + bias2_ref[0:1, :], text_cols(col + 2 * SEC)),
        ]
        top = functools.reduce(
            jnp.maximum, [jnp.max(sc, axis=1, keepdims=True) for sc, _ in parts]
        ) * C2
        ws = [jnp.exp2(sc * C2 - top) for sc, _ in parts]
        total = sum(jnp.sum(w, axis=1, keepdims=True) for w in ws)
        mixed = sum(pv(w, v) for w, (_, v) in zip(ws, parts))
        Pt[:, :, :, hcol(hh * HEAD)] = mixed.astype(jnp.bfloat16).reshape(4, 4, 16, HEAD)
        here = lax.broadcasted_iota(jnp.int32, (256, HEAD), 1) == hh
        for n, v in ((0, top), (1, total)):
            old = PS[n].reshape(256, HEAD)
            PS[n] = jnp.where(here, v, old).reshape(4, 4, 16, HEAD)
        return carry

    def r1(i, yy):
        device = dev(x, up(y, i), z, core)
        return (
            remote(Pt.at[yy], RB1.at[i - 1], r_s.at[0, i], r_r.at[0, i], device),
            remote(PS.at[:, yy], RS1.at[i - 1], r_s.at[1, i], r_r.at[1, i], device),
        )

    def r2(i, zz):
        device = dev(x, y, up(z, i), core)
        return (
            remote(P2.at[zz], RB2.at[i - 1], r_s.at[2, i], r_r.at[2, i], device),
            remote(S2.at[:, zz], RS2.at[i - 1], r_s.at[3, i], r_r.at[3, i], device),
        )

    def r3(i):
        device = dev(up(x, i), y, z, core)
        return (
            remote(P3, RB3.at[i - 1], r_s.at[4, i], r_r.at[4, i], device),
            remote(S3, RS3.at[i - 1], r_s.at[5, i], r_r.at[5, i], device),
        )

    for i in range(1, 4):
        for cp in r1(i, up(y, i)):
            cp.start()
    send_loop([(FAR, has_far)])

    def merge1():
        for i in range(1, 4):
            for cp in r1(i, up(y, i)):
                cp.wait_recv()
        stats = [(PS[0, y].reshape(64, HEAD), PS[1, y].reshape(64, HEAD))]
        stats += [(RS1[i, 0].reshape(64, HEAD), RS1[i, 1].reshape(64, HEAD)) for i in range(3)]

        def own(h):
            return Pt[y, :, :, h * HEAD : (h + 1) * HEAD].reshape(64, HEAD)

        def got(i):
            return lambda h: RB1[i, :, :, h * HEAD : (h + 1) * HEAD].reshape(64, HEAD)

        def out(h, v):
            P2[:, :, h * HEAD : (h + 1) * HEAD] = v.reshape(4, 16, HEAD)

        def out_stats(m, l):
            S2[0] = m.reshape(4, 16, HEAD)
            S2[1] = l.reshape(4, 16, HEAD)

        merge([own] + [got(i) for i in range(3)], stats, out, out_stats, False)
        for i in range(1, 4):
            for cp in r2(i, up(z, i)):
                cp.start()

    def merge2():
        for i in range(1, 4):
            for cp in r2(i, up(z, i)):
                cp.wait_recv()
        stats = [(S2[0, z], S2[1, z])] + [(RS2[i, 0], RS2[i, 1]) for i in range(3)]

        def own(h):
            return P2[z, :, h * HEAD : (h + 1) * HEAD]

        def got(i):
            return lambda h: RB2[i, :, h * HEAD : (h + 1) * HEAD]

        def out(h, v):
            P3[:, h * HEAD : (h + 1) * HEAD] = v

        def out_stats(m, l):
            S3[0] = m
            S3[1] = l

        merge([own] + [got(i) for i in range(3)], stats, out, out_stats, False)
        for i in range(1, 4):
            for cp in r3(i):
                cp.start()

    fcols = pl.ds(pl.multiple_of(core * (D // 2), 128), D // 2)
    ocols = pl.ds(pl.multiple_of((1 - core) * (D // 2), 128), D // 2)
    f_out = remote(full.at[:, fcols], full.at[:, fcols], r_s.at[6, 0], r_r.at[6, 0], (pair_t, s))
    f_in = remote(full.at[:, ocols], full.at[:, ocols], r_s.at[6, 0], r_r.at[6, 0], (pair_t, s))

    def merge3():
        for i in range(1, 4):
            for cp in r3(i):
                cp.wait_recv()
        stats = [(S3[0], S3[1])] + [(RS3[i, 0], RS3[i, 1]) for i in range(3)]

        def own(h):
            return P3[:, h * HEAD : (h + 1) * HEAD]

        def got(i):
            return lambda h: RB3[i, :, h * HEAD : (h + 1) * HEAD]

        def out(h, v):
            full[:, hcol(core * (D // 2) + h * HEAD)] = v

        merge([own] + [got(i) for i in range(3)], stats, out, None, True)
        f_out.start()

    half_in.wait_recv()
    number = [(pair_t, s), (far_t, s), (t, s - 1), (t, s + 1)]
    exists = [None, has_far, has_left, has_right]
    seen = []
    for k in range(4):
        tile = number[k][0] * 8 + number[k][1]
        hit = jnp.int32(0)
        for n in range(4):
            hit = hit + jnp.where(pat_ref[n] == tile, 1, 0)
        if exists[k] is not None:
            hit = hit * jnp.where(exists[k], 1, 0)
        seen.append(hit)
    slots = [PAIR] + [jnp.where(exists[k], k, OWN) for k in (FAR, LEFT, RIGHT)]
    drop = [jnp.where(h > 0, 0.0, NEG).astype(jnp.float32) for h in seen]

    def relay(c):
        def forward(cond, k_sem, slot, to_slot, device):
            @pl.when(cond)
            def _():
                for sec in range(2):
                    halo(0, c, sec, kv_hbm, slot, device).wait_recv()
                    remote(
                        buf.at[slot, :, cols(c, sec)], buf.at[to_slot, :, cols(c, sec)],
                        fwd_s.at[k_sem], hr.at[to_slot, c, sec], device,
                    ).start()

        forward(s == 7, 0, RIGHT, LEFT, (t, 4))
        forward(s == 0, 0, LEFT, RIGHT, (t, 3))
        forward(far_relay, 1, FAR, FAR, (relay_fin_t, s))

    def video(c):
        for k in (FAR, LEFT, RIGHT):

            @pl.when(exists[k])
            def _():
                for sec in range(2):
                    halo(0, c, sec, kv_hbm, k, (t, s)).wait_recv()

        for hh in range(2):
            col = c * CW + hh * HEAD
            tcol = (c // 3) * TQ + lax.rem(c, 3) * CW + hh * HEAD
            qh = q[:, hcol(col)]
            sc = [qk(qh, buf[OWN, :, hcol(col)])]
            sc += [qk(qh, buf[slots[k], :, hcol(col)]) for k in range(4)]
            sc.append(qk(qh, text_cols(tcol + SEC)) + bias_ref[0:1, :])
            tops = [jnp.max(v, axis=1, keepdims=True) for v in sc]
            for k in range(4):
                tops[1 + k] = tops[1 + k] + drop[k]
            top = functools.reduce(jnp.maximum, tops) * C2
            lows = [top] + [top - drop[k] for k in range(4)] + [top]
            ws = [jnp.exp2(v * C2 - low) for v, low in zip(sc, lows)]
            total = sum(jnp.sum(w, axis=1, keepdims=True) for w in ws)
            vs = [buf[OWN, :, hcol(col + D)]]
            vs += [buf[slots[k], :, hcol(col + D)] for k in range(4)]
            vs.append(text_cols(tcol + 2 * SEC))
            mixed = sum(pv(w, v) for w, v in zip(ws, vs))
            video_ref[:, hcol(col)] = (mixed / total).astype(jnp.bfloat16)

    @functools.partial(lax.fori_loop, 0, CHUNKS, init_val=0)
    def _(c, carry):
        @pl.when(lax.rem(c, 2) == 0)
        def _():
            relay(c + 1)

        pl.when(c == 6)(merge1)
        pl.when(c == 9)(merge2)
        video(c)
        return carry

    merge3()
    f_in.wait_recv()
    pick_r = lax.broadcasted_iota(jnp.int32, (16, 16), 0)
    pick_c = lax.broadcasted_iota(jnp.int32, (16, 16), 1)
    pick = jnp.where(pick_c == pick_r + 2 * g, 1.0, 0.0).astype(jnp.bfloat16)
    chosen = jnp.dot(pick, full[...], preferred_element_type=jnp.float32)
    tout_ref[...] = chosen[:2].astype(jnp.bfloat16)

    for i in range(1, 8):
        g_copy(i, g).wait_send()
    for step in range(2):
        for i in range(1, 4):
            for half in range(2):
                step_copy(step, half, i, y, z).wait_send()
    half_out.wait_send()
    pair_copy().wait_send()

    def drain(cond, sem, width):
        @pl.when(cond)
        def _():
            ref = buf.at[OWN, :, pl.ds(0, width)]
            remote(ref, ref, sem, hr.at[0, 0, 0], (pair_t, s)).wait_send()

    drain(has_far, hs.at[FAR], 2 * D)
    drain(has_left, hs.at[LEFT], 2 * D)
    drain(has_right, hs.at[RIGHT], 2 * D)
    drain(jnp.logical_or(s == 0, s == 7), fwd_s.at[0], D)
    drain(far_relay, fwd_s.at[1], D)
    for i in range(1, 4):
        for cp in r1(i, up(y, i)) + r2(i, up(z, i)) + r3(i):
            cp.wait_send()
    f_out.wait_send()


def local(video_q, video_kv, text_qkv, text_mask, pattern):
    bf, f32 = jnp.bfloat16, jnp.float32
    dma = pltpu.SemaphoreType.DMA
    vm = pltpu.VMEM
    whole = pl.BlockSpec(memory_space=pltpu.VMEM)
    hbm = pl.BlockSpec(memory_space=pl.ANY)
    scratch = [
        vm((5, TILE, 2 * D), bf),
        vm((TILE, D), bf),
        vm((16, TCOLS // 8), bf),
        vm((8, 16, TCOLS // 8), bf),
        vm((4, 4, 16, TCOLS), bf),
        vm((8, 256), f32),
        vm((8, 256), f32),
        vm((4, 4, 16, D // 2), bf),
        vm((2, 4, 4, 16, HEAD), f32),
        vm((3, 4, 16, D // 2), bf),
        vm((3, 2, 4, 16, HEAD), f32),
        vm((4, 16, D // 2), bf),
        vm((2, 4, 16, HEAD), f32),
        vm((3, 16, D // 2), bf),
        vm((3, 2, 16, HEAD), f32),
        vm((16, D // 2), bf),
        vm((2, 16, HEAD), f32),
        vm((3, 16, D // 2), bf),
        vm((3, 2, 16, HEAD), f32),
        vm((16, D), bf),
        dma((2,)), dma((8,)), dma((8,)), dma((2, 2, 4)), dma((2, 2, 4)),
        dma, dma, dma, dma, dma((4,)), dma((4, CHUNKS, 2)), dma((2,)), dma((7, 4)), dma((7, 4)),
    ]
    video_out, text_out = pl.pallas_call(
        kernel,
        out_shape=(jax.ShapeDtypeStruct((TILE, D), bf), jax.ShapeDtypeStruct((2, D), bf)),
        in_specs=[hbm, hbm, whole, whole, pl.BlockSpec(memory_space=pltpu.SMEM)],
        out_specs=(whole, whole),
        scratch_shapes=scratch,
        compiler_params=pltpu.CompilerParams(
            collective_id=0, has_side_effects=True, vmem_limit_bytes=58 * 2**20
        ),
        cost_estimate=pl.CostEstimate(
            flops=6 * 10**9, bytes_accessed=10**7, transcendentals=12 * 10**6
        ),
    )(video_q[0, 0], video_kv[0, 0], text_qkv, text_mask.reshape(1, 256), pattern.reshape(4))
    return video_out[None, None], text_out


def solution(mesh):
    in_specs = (
        P("ta", "sa", None, None),
        P("ta", "sa", None, None),
        P(("ta", "sa"), None),
        P(),
        P("ta", "sa", None),
    )
    out_specs = (P("ta", "sa", None, None), P(("ta", "sa"), None))
    return jax.shard_map(local, mesh=mesh, in_specs=in_specs, out_specs=out_specs, check_vma=False)
```

```python
import functools
import math

import jax
import jax.numpy as jnp
from jax import lax
from jax.experimental import pallas as pl
from jax.experimental.pallas import tpu as pltpu
from jax.sharding import PartitionSpec as P

HEAD = 128
D = 3072
TILE = 256
HEADS = 24
HALF = 12
CHUNKS = 12
CW = D // CHUNKS
TCOLS = 3 * D
THALF = TCOLS // 2
TQ = THALF // 2
SEC = TQ // 3
MESH = pl.DeviceIdType.MESH
C2 = math.log2(math.e) / math.sqrt(HEAD)
NEG = -1e30
FAR_EARLY, X_EARLY, AT1, AT2 = 3, 10, 1, 5
PAIR, FAR, LEFT, RIGHT, OWN = 0, 1, 2, 3, 4


def qk(q, k):
    return lax.dot_general(q, k, (((1,), (1,)), ((), ())), preferred_element_type=jnp.float32)


def pv(p, v):
    return jnp.dot(p.astype(jnp.bfloat16), v, preferred_element_type=jnp.float32)


def merge(parts, stats, out, out_stats, last):
    top = functools.reduce(jnp.maximum, [m for m, _ in stats])
    weights = [jnp.exp2(m - top) for m, _ in stats]
    total = sum(w * l for w, (_, l) in zip(weights, stats))
    if last:
        weights = [w / total for w in weights]
    else:
        out_stats(top, total)
    for h in range(HALF):
        mixed = sum(
            w[..., h : h + 1] * part(h).astype(jnp.float32) for w, part in zip(weights, parts)
        )
        out(h, mixed.astype(jnp.bfloat16))


def kernel(
    q_hbm, kv_hbm, text_ref, mask_ref, pat_ref, video_ref, tout_ref,
    buf, q, stage, G, T, bias_ref, bias2_ref, Pt, PS, RB1, RS1, P2, S2, RB2, RS2, P3, S3, RB3, RS3, TT, ST, full,
    lsem, g_s, g_r, a_s, a_r, b_s, b_r, x_s, x_r, pair_s, pair_r, hs, hr, fwd_s, r_s, r_r,
):
    t = lax.axis_index("ta")
    s = lax.axis_index("sa")
    core = lax.rem(t, 2)
    y = lax.rem(t // 2, 4)
    x = lax.rem(s, 4)
    z = (t // 8) * 2 + s // 4
    g = x * 2 + core

    def dev(x_, y_, z_, core_):
        return ((z_ // 2) * 8 + y_ * 2 + core_, lax.rem(z_, 2) * 4 + x_)

    def up(v, i, n=4):
        return lax.rem(v + i, n)

    pair_t = t + 1 - 2 * core
    far_t = t + 2 * core - 1
    has_far = jnp.logical_and(far_t >= 0, far_t <= 15)
    has_left = s > 0
    has_right = s < 7
    far_cross = jnp.logical_or(t == 7, t == 8)
    far_relay = jnp.logical_or(t == 0, t == 15)

    def g_peer(i):
        gg = up(g, i, 8)
        return dev(gg // 2, y, z, lax.rem(gg, 2))

    own_copy = pltpu.make_async_copy(kv_hbm, buf.at[OWN], lsem.at[0])
    q_copy = pltpu.make_async_copy(q_hbm, q, lsem.at[1])
    own_copy.start()
    q_copy.start()
    barrier = pltpu.get_barrier_semaphore()

    def greet(device):
        pl.semaphore_signal(barrier, inc=1, device_id=device, device_id_type=MESH)

    for i in range(1, 8):
        greet(g_peer(i))
    for i in range(1, 4):
        greet(dev(x, y, up(z, i), core))
        greet(dev(x, up(y, i), z, core))
    extra = [
        (has_far, (far_t, s)),
        (t == 15, (8, s)),
        (t == 8, (15, s)),
        (t == 0, (7, s)),
        (t == 7, (0, s)),
    ]
    for cond, device in extra:

        @pl.when(cond)
        def _():
            greet(device)

    rows = text_ref[...].astype(jnp.float32)
    w8 = TCOLS // 8
    stage[...] = jnp.concatenate(
        [rows[:, j * w8 : (j + 1) * w8] for j in range(8)], axis=0
    ).astype(jnp.bfloat16)

    pl.semaphore_wait(barrier, 13 + sum(jnp.where(cond, 1, 0) for cond, _ in extra))

    def remote(src, dst, ssem, rsem, device):
        return pltpu.make_async_remote_copy(
            src_ref=src, dst_ref=dst, send_sem=ssem, recv_sem=rsem,
            device_id=device, device_id_type=MESH,
        )

    def g_copy(i, slot):
        return remote(stage, G.at[slot], g_s.at[i], g_r.at[i], g_peer(i))

    for i in range(1, 8):
        g_copy(i, g).start()
    G[pl.ds(g, 1)] = stage[...][None]

    def cols(c, sec):
        return pl.ds(pl.multiple_of(c * CW + sec * D, 128), CW)

    def halo(k, c, sec, src, slot, device):
        return remote(
            src.at[:, cols(c, sec)], buf.at[slot, :, cols(c, sec)],
            hs.at[k], hr.at[slot, c, sec], device,
        )

    def send_halo(k, c):
        odd = lax.rem(c, 2) == 1
        if k == FAR:
            out_t = jnp.where((t == 7) == odd, 15, 0)
            device = (jnp.where(far_cross, out_t, far_t), s)
            slot = FAR
        else:
            edge = 3 if k == RIGHT else 4
            out_s = jnp.where((s == 3) == odd, 7, 0)
            normal = s + 1 if k == RIGHT else s - 1
            device = (t, jnp.where(s == edge, out_s, normal))
            slot = jnp.where(s == edge, jnp.where(out_s == 7, RIGHT, LEFT), LEFT if k == RIGHT else RIGHT)
        for sec in range(2):
            halo(k, c, sec, kv_hbm, slot, device).start()

    def send_loop(first, last, conds, stride=1):
        @functools.partial(lax.fori_loop, 0, (last - first + stride - 1) // stride, init_val=0)
        def _(n, carry):
            c = first + n * stride
            for k, cond in conds:

                @pl.when(cond)
                def _():
                    send_halo(k, c)

            return carry

    along_x = [
        (LEFT, jnp.logical_and(has_left, s != 4)),
        (RIGHT, jnp.logical_and(has_right, s != 3)),
    ]
    crossing = [(LEFT, s == 4), (RIGHT, s == 3)]
    send_loop(0, 1, along_x + crossing)
    send_loop(0, FAR_EARLY, [(FAR, has_far)])
    send_loop(1, 2, crossing)
    send_loop(1, X_EARLY, along_x)
    send_loop(2, CHUNKS, crossing, 2)

    def pair_copy():
        return remote(kv_hbm, buf.at[PAIR], pair_s, pair_r, (pair_t, s))

    pair_copy().start()

    def forward(cond, c, sem, slot, to_slot, device):
        @pl.when(cond)
        def _():
            for sec in range(2):
                halo(0, c, sec, kv_hbm, slot, device).wait_recv()
                remote(
                    buf.at[slot, :, cols(c, sec)], buf.at[to_slot, :, cols(c, sec)],
                    sem, hr.at[to_slot, c, sec], device,
                ).start()

    def relay_x(c, on=True):
        odd = lax.rem(c, 2) == 1
        to_s = jnp.where((s == 7) == odd, 4, 3)
        edge = jnp.logical_and(jnp.logical_or(s == 0, s == 7), on)
        slot = jnp.where(s == 7, RIGHT, LEFT)
        forward(edge, c, fwd_s.at[0], slot, jnp.where(to_s == 4, LEFT, RIGHT), (t, to_s))

    def relay_t(c, on=True):
        odd = lax.rem(c, 2) == 1
        to_t = jnp.where((t == 15) == odd, 8, 7)
        forward(jnp.logical_and(far_relay, on), c, fwd_s.at[1], FAR, FAR, (to_t, s))

    for i in range(1, 8):
        g_copy(i, up(g, 8 - i, 8)).wait_recv()
    r_ = lax.broadcasted_iota(jnp.int32, (128, 128), 0)
    c_ = lax.broadcasted_iota(jnp.int32, (128, 128), 1)
    swap = (r_ // 16 == lax.rem(c_, 16) // 2) & (lax.rem(r_, 16) // 2 == c_ // 16)
    swap = swap & (lax.rem(r_, 2) == lax.rem(c_, 2))
    mixed_rows = jnp.dot(
        jnp.where(swap, 1.0, 0.0).astype(jnp.bfloat16),
        G[...].reshape(128, w8),
        preferred_element_type=jnp.float32,
    ).astype(jnp.bfloat16)
    def place(cc):
        for sec in range(3):
            for n in range(4):
                p = (sec * 4 + cc * 2) * 2 + n
                j, off = p // 3, (p % 3) * 384
                col = cc * THALF + (n // 2) * TQ + sec * SEC + (n % 2) * 384
                T[pl.ds(y, 1), pl.ds(z, 1), :, col : col + 384] = mixed_rows[
                    16 * j : 16 * j + 16, off : off + 384
                ][None, None]

    pl.when(core == 0)(lambda: place(0))
    pl.when(core == 1)(lambda: place(1))

    base = core * THALF

    def step_copy(step, part, half, i, yy, zz):
        along_z = (step == 0) == (half == 0)
        width = (TQ, SEC, 2 * SEC)[part]
        cs = pl.ds(pl.multiple_of(base + half * TQ + (SEC if part == 2 else 0), 128), width)
        if step == 0:
            ref = T.at[yy, zz, :, cs]
        elif half == 0:
            ref = T.at[yy, :, :, cs]
        else:
            ref = T.at[:, zz, :, cs]
        device = dev(x, y, up(z, i), core) if along_z else dev(x, up(y, i), z, core)
        return remote(ref, ref, a_s.at[part, half, i], a_r.at[part, half, i], device)

    def step_starts(step, part):
        for i in (2, 1, 3):
            for half in range(2):
                step_copy(step, part, half, i, y, z).start()

    def step_waits(step, part):
        for half in range(2):
            along_z = (step == 0) == (half == 0)
            for i in range(1, 4):
                if along_z:
                    step_copy(step, part, half, i, y, up(z, 4 - i)).wait_recv()
                else:
                    step_copy(step, part, half, i, up(y, 4 - i), z).wait_recv()

    step_starts(0, 0)
    step_waits(0, 0)
    step_starts(1, 1)
    step_starts(1, 2)
    send_loop(3, 6, crossing, 2)
    send_loop(3, CHUNKS, [(FAR, far_cross)], 2)

    r_ = lax.broadcasted_iota(jnp.int32, (256, 256), 0)
    c_ = lax.broadcasted_iota(jnp.int32, (256, 256), 1)
    by, bz, bx = c_ // 64, lax.rem(c_ // 16, 4), lax.rem(c_, 16) // 4
    bc, bi = lax.rem(c_ // 2, 2), lax.rem(c_, 2)
    row_of = (((bz // 2) * 8 + by * 2 + bc) * 8 + lax.rem(bz, 2) * 4 + bx) * 2 + bi
    valid = jnp.where(mask_ref[...] == 1, 1.0, 0.0)
    hot = jnp.where(r_ == row_of, 1.0, 0.0).astype(jnp.bfloat16)
    kept = jnp.dot(
        jnp.broadcast_to(valid, (8, 256)).astype(jnp.bfloat16), hot,
        preferred_element_type=jnp.float32,
    )
    bias = jnp.where(kept > 0.5, 0.0, NEG)
    bias_ref[...] = bias
    lane = lax.broadcasted_iota(jnp.int32, (8, 256), 1)
    bias2_ref[...] = jnp.where(lane // 64 == x, bias, NEG)

    own_copy.wait()
    q_copy.wait()
    pair_copy().wait_recv()
    step_waits(1, 1)
    for c in (0, 2, 4):
        relay_x(c)
    for c in (0, 2):
        relay_t(c)
    PS[...] = jnp.zeros_like(PS)

    def hcol(v):
        return pl.ds(pl.multiple_of(v, 128), HEAD)

    def text_cols(col):
        return T[:, :, :, hcol(col)].reshape(256, HEAD)

    @functools.partial(lax.fori_loop, 0, HALF, init_val=0)
    def _(hh, carry):
        col = base + (hh // 6) * TQ + lax.rem(hh, 6) * HEAD
        kcol = core * (D // 2) + hh * HEAD
        qx = text_cols(col)
        parts = [
            (qk(qx, buf[OWN, :, hcol(kcol)]), buf[OWN, :, hcol(kcol + D)]),
            (qk(qx, buf[PAIR, :, hcol(kcol)]), buf[PAIR, :, hcol(kcol + D)]),
        ]
        top = functools.reduce(
            jnp.maximum, [jnp.max(sc, axis=1, keepdims=True) for sc, _ in parts]
        ) * C2
        ws = [jnp.exp2(sc * C2 - top) for sc, _ in parts]
        total = sum(jnp.sum(w, axis=1, keepdims=True) for w in ws)
        mixed = sum(pv(w, v) for w, (_, v) in zip(ws, parts))
        Pt[:, :, :, hcol(hh * HEAD)] = mixed.astype(jnp.bfloat16).reshape(4, 4, 16, HEAD)
        here = lax.broadcasted_iota(jnp.int32, (256, HEAD), 1) == hh
        for n, v in ((0, top), (1, total)):
            old = PS[n].reshape(256, HEAD)
            PS[n] = jnp.where(here, v, old).reshape(4, 4, 16, HEAD)
        return carry

    def r1(i, yy):
        device = dev(x, up(y, i), z, core)
        return (
            remote(Pt.at[yy], RB1.at[i - 1], r_s.at[0, i], r_r.at[0, i], device),
            remote(PS.at[:, yy], RS1.at[i - 1], r_s.at[1, i], r_r.at[1, i], device),
        )

    def r2(i, zz):
        device = dev(x, y, up(z, i), core)
        return (
            remote(P2.at[zz], RB2.at[i - 1], r_s.at[2, i], r_r.at[2, i], device),
            remote(S2.at[:, zz], RS2.at[i - 1], r_s.at[3, i], r_r.at[3, i], device),
        )

    def r3(i):
        device = dev(up(x, i), y, z, core)
        return (
            remote(P3, RB3.at[i - 1], r_s.at[4, i], r_r.at[4, i], device),
            remote(S3, RS3.at[i - 1], r_s.at[5, i], r_r.at[5, i], device),
        )

    for i in range(1, 4):
        for cp in r1(i, up(y, i)):
            cp.start()
    send_loop(FAR_EARLY, CHUNKS, [(FAR, jnp.logical_and(has_far, jnp.logical_not(far_cross)))])
    send_loop(4, CHUNKS, [(FAR, far_cross)], 2)

    step_waits(1, 2)

    def half_copy(ab, which):
        cs = pl.ds(pl.multiple_of(which * THALF + ab * TQ + SEC, 128), 2 * SEC)
        ref = T.at[:, :, :, cs]
        return remote(ref, ref, b_s.at[ab], b_r.at[ab], (pair_t, s))

    for ab in range(2):
        half_copy(ab, core).start()

    ST[...] = jnp.zeros_like(ST)

    @functools.partial(lax.fori_loop, 0, HALF, init_val=0)
    def _(hh, carry):
        col = base + (hh // 6) * TQ + lax.rem(hh, 6) * HEAD
        sc = qk(T[y, z, :, hcol(col)], text_cols(col + SEC)) + bias2_ref[0:1, :]
        top = jnp.max(sc, axis=1, keepdims=True) * C2
        w = jnp.exp2(sc * C2 - top)
        TT[:, hcol(hh * HEAD)] = pv(w, text_cols(col + 2 * SEC)).astype(jnp.bfloat16)
        here = lax.broadcasted_iota(jnp.int32, (16, HEAD), 1) == hh
        for n, v in ((0, top), (1, jnp.sum(w, axis=1, keepdims=True))):
            ST[n] = jnp.where(here, v, ST[n])
        return carry


    def merge1():
        for i in range(1, 4):
            for cp in r1(i, up(y, i)):
                cp.wait_recv()
        stats = [(PS[0, y].reshape(64, HEAD), PS[1, y].reshape(64, HEAD))]
        stats += [(RS1[i, 0].reshape(64, HEAD), RS1[i, 1].reshape(64, HEAD)) for i in range(3)]

        def own(h):
            return Pt[y, :, :, h * HEAD : (h + 1) * HEAD].reshape(64, HEAD)

        def got(i):
            return lambda h: RB1[i, :, :, h * HEAD : (h + 1) * HEAD].reshape(64, HEAD)

        def out(h, v):
            P2[:, :, h * HEAD : (h + 1) * HEAD] = v.reshape(4, 16, HEAD)

        def out_stats(m, l):
            S2[0] = m.reshape(4, 16, HEAD)
            S2[1] = l.reshape(4, 16, HEAD)

        merge([own] + [got(i) for i in range(3)], stats, out, out_stats, False)
        for i in range(1, 4):
            for cp in r2(i, up(z, i)):
                cp.start()

    def merge2():
        for i in range(1, 4):
            for cp in r2(i, up(z, i)):
                cp.wait_recv()
        stats = [(S2[0, z], S2[1, z])] + [(RS2[i, 0], RS2[i, 1]) for i in range(3)]
        stats.append((ST[0], ST[1]))

        def local_text(h):
            return TT[:, h * HEAD : (h + 1) * HEAD]

        def own(h):
            return P2[z, :, h * HEAD : (h + 1) * HEAD]

        def got(i):
            return lambda h: RB2[i, :, h * HEAD : (h + 1) * HEAD]

        def out(h, v):
            P3[:, h * HEAD : (h + 1) * HEAD] = v

        def out_stats(m, l):
            S3[0] = m
            S3[1] = l

        merge([own] + [got(i) for i in range(3)] + [local_text], stats, out, out_stats, False)
        for i in range(1, 4):
            for cp in r3(i):
                cp.start()
        send_loop(X_EARLY, CHUNKS, along_x)

    fcols = pl.ds(pl.multiple_of(core * (D // 2), 128), D // 2)
    ocols = pl.ds(pl.multiple_of((1 - core) * (D // 2), 128), D // 2)
    f_out = remote(full.at[:, fcols], full.at[:, fcols], r_s.at[6, 0], r_r.at[6, 0], (pair_t, s))
    f_in = remote(full.at[:, ocols], full.at[:, ocols], r_s.at[6, 0], r_r.at[6, 0], (pair_t, s))

    def merge3():
        for i in range(1, 4):
            for cp in r3(i):
                cp.wait_recv()
        stats = [(S3[0], S3[1])] + [(RS3[i, 0], RS3[i, 1]) for i in range(3)]

        def own(h):
            return P3[:, h * HEAD : (h + 1) * HEAD]

        def got(i):
            return lambda h: RB3[i, :, h * HEAD : (h + 1) * HEAD]

        def out(h, v):
            full[:, hcol(core * (D // 2) + h * HEAD)] = v

        merge([own] + [got(i) for i in range(3)], stats, out, None, True)
        f_out.start()

    for ab in range(2):
        half_copy(ab, 1 - core).wait_recv()
    number = [(pair_t, s), (far_t, s), (t, s - 1), (t, s + 1)]
    exists = [None, has_far, has_left, has_right]
    seen = []
    for k in range(4):
        tile = number[k][0] * 8 + number[k][1]
        hit = jnp.int32(0)
        for n in range(4):
            hit = hit + jnp.where(pat_ref[n] == tile, 1, 0)
        if exists[k] is not None:
            hit = hit * jnp.where(exists[k], 1, 0)
        seen.append(hit)
    slots = [PAIR] + [jnp.where(exists[k], k, OWN) for k in (FAR, LEFT, RIGHT)]
    drop = [jnp.where(h > 0, 0.0, NEG).astype(jnp.float32) for h in seen]

    def video(c):
        for k in (FAR, LEFT, RIGHT):

            @pl.when(exists[k])
            def _():
                for sec in range(2):
                    halo(0, c, sec, kv_hbm, k, (t, s)).wait_recv()

        for hh in range(2):
            col = c * CW + hh * HEAD
            tcol = (c // 3) * TQ + lax.rem(c, 3) * CW + hh * HEAD
            qh = q[:, hcol(col)]
            sc = [qk(qh, buf[OWN, :, hcol(col)])]
            sc += [qk(qh, buf[slots[k], :, hcol(col)]) for k in range(4)]
            sc.append(qk(qh, text_cols(tcol + SEC)) + bias_ref[0:1, :])
            tops = [jnp.max(v, axis=1, keepdims=True) for v in sc]
            for k in range(4):
                tops[1 + k] = tops[1 + k] + drop[k]
            top = functools.reduce(jnp.maximum, tops) * C2
            lows = [top] + [top - drop[k] for k in range(4)] + [top]
            ws = [jnp.exp2(v * C2 - low) for v, low in zip(sc, lows)]
            total = sum(jnp.sum(w, axis=1, keepdims=True) for w in ws)
            vs = [buf[OWN, :, hcol(col + D)]]
            vs += [buf[slots[k], :, hcol(col + D)] for k in range(4)]
            vs.append(text_cols(tcol + 2 * SEC))
            mixed = sum(pv(w, v) for w, v in zip(ws, vs))
            video_ref[:, hcol(col)] = (mixed / total).astype(jnp.bfloat16)

    relay_x(1)
    relay_t(1)

    @functools.partial(lax.fori_loop, 0, CHUNKS, init_val=0)
    def _(c, carry):
        odd = lax.rem(c, 2)
        relay_x(jnp.where(odd == 1, c + 2, c + 6), c < jnp.where(odd == 1, 10, 6))
        relay_t(c + 3, c < CHUNKS - 3)

        @pl.when(jnp.logical_and(odd == 0, c < 6))
        def _():
            for k, cond in crossing:

                @pl.when(cond)
                def _():
                    send_halo(k, c + 7)

        pl.when(c == AT1)(merge1)
        pl.when(c == AT2)(merge2)
        pl.when(c == CHUNKS - 1)(merge3)
        video(c)
        return carry

    f_in.wait_recv()
    pick_r = lax.broadcasted_iota(jnp.int32, (16, 16), 0)
    pick_c = lax.broadcasted_iota(jnp.int32, (16, 16), 1)
    pick = jnp.where(pick_c == pick_r + 2 * g, 1.0, 0.0).astype(jnp.bfloat16)
    chosen = jnp.dot(pick, full[...], preferred_element_type=jnp.float32)
    tout_ref[...] = chosen[:2].astype(jnp.bfloat16)

    for i in range(1, 8):
        g_copy(i, g).wait_send()
    for part in range(3):
        for i in range(1, 4):
            for half in range(2):
                step_copy(min(part, 1), part, half, i, y, z).wait_send()
    for ab in range(2):
        half_copy(ab, core).wait_send()
    pair_copy().wait_send()

    def drain(cond, sem, width):
        @pl.when(cond)
        def _():
            ref = buf.at[OWN, :, pl.ds(0, width)]
            remote(ref, ref, sem, hr.at[0, 0, 0], (pair_t, s)).wait_send()

    drain(has_far, hs.at[FAR], 2 * D)
    drain(has_left, hs.at[LEFT], 2 * D)
    drain(has_right, hs.at[RIGHT], 2 * D)
    drain(jnp.logical_or(s == 0, s == 7), fwd_s.at[0], 2 * D)
    drain(far_relay, fwd_s.at[1], 2 * D)
    for i in range(1, 4):
        for cp in r1(i, up(y, i)) + r2(i, up(z, i)) + r3(i):
            cp.wait_send()
    f_out.wait_send()


def local(video_q, video_kv, text_qkv, text_mask, pattern):
    bf, f32 = jnp.bfloat16, jnp.float32
    dma = pltpu.SemaphoreType.DMA
    vm = pltpu.VMEM
    whole = pl.BlockSpec(memory_space=pltpu.VMEM)
    hbm = pl.BlockSpec(memory_space=pl.ANY)
    scratch = [
        vm((5, TILE, 2 * D), bf),
        vm((TILE, D), bf),
        vm((16, TCOLS // 8), bf),
        vm((8, 16, TCOLS // 8), bf),
        vm((4, 4, 16, TCOLS), bf),
        vm((8, 256), f32),
        vm((8, 256), f32),
        vm((4, 4, 16, D // 2), bf),
        vm((2, 4, 4, 16, HEAD), f32),
        vm((3, 4, 16, D // 2), bf),
        vm((3, 2, 4, 16, HEAD), f32),
        vm((4, 16, D // 2), bf),
        vm((2, 4, 16, HEAD), f32),
        vm((3, 16, D // 2), bf),
        vm((3, 2, 16, HEAD), f32),
        vm((16, D // 2), bf),
        vm((2, 16, HEAD), f32),
        vm((3, 16, D // 2), bf),
        vm((3, 2, 16, HEAD), f32),
        vm((16, D // 2), bf),
        vm((2, 16, HEAD), f32),
        vm((16, D), bf),
        dma((2,)), dma((8,)), dma((8,)), dma((3, 2, 4)), dma((3, 2, 4)),
        dma((2,)), dma((2,)), dma, dma, dma, dma, dma((4,)), dma((4, CHUNKS, 2)), dma((2,)), dma((7, 4)), dma((7, 4)),
    ]
    video_out, text_out = pl.pallas_call(
        kernel,
        out_shape=(jax.ShapeDtypeStruct((TILE, D), bf), jax.ShapeDtypeStruct((2, D), bf)),
        in_specs=[hbm, hbm, whole, whole, pl.BlockSpec(memory_space=pltpu.SMEM)],
        out_specs=(whole, whole),
        scratch_shapes=scratch,
        compiler_params=pltpu.CompilerParams(
            collective_id=0, has_side_effects=True, vmem_limit_bytes=58 * 2**20
        ),
        cost_estimate=pl.CostEstimate(
            flops=6 * 10**9, bytes_accessed=10**7, transcendentals=12 * 10**6
        ),
    )(video_q[0, 0], video_kv[0, 0], text_qkv, text_mask.reshape(1, 256), pattern.reshape(4))
    return video_out[None, None], text_out


def solution(mesh):
    in_specs = (
        P("ta", "sa", None, None),
        P("ta", "sa", None, None),
        P(("ta", "sa"), None),
        P(),
        P("ta", "sa", None),
    )
    out_specs = (P("ta", "sa", None, None), P(("ta", "sa"), None))
    return jax.shard_map(local, mesh=mesh, in_specs=in_specs, out_specs=out_specs, check_vma=False)
```

```python
import functools
import math

import jax
import jax.numpy as jnp
from jax import lax
from jax.experimental import pallas as pl
from jax.experimental.pallas import tpu as pltpu
from jax.sharding import PartitionSpec as P

HEAD = 128
D = 3072
TILE = 256
HEADS = 24
HALF = 12
CHUNKS = 12
CW = D // CHUNKS
TCOLS = 3 * D
THALF = TCOLS // 2
TQ = THALF // 2
SEC = TQ // 3
MESH = pl.DeviceIdType.MESH
C2 = math.log2(math.e) / math.sqrt(HEAD)
NEG = -1e30
FAR_EARLY, X_EARLY, AT1, AT2 = 3, 11, 1, 6
PAIR, FAR, LEFT, RIGHT, OWN = 0, 1, 2, 3, 4


def qk(q, k):
    return lax.dot_general(q, k, (((1,), (1,)), ((), ())), preferred_element_type=jnp.float32)


def pv(p, v):
    return jnp.dot(p.astype(jnp.bfloat16), v, preferred_element_type=jnp.float32)


def merge(parts, stats, out, out_stats, last):
    top = functools.reduce(jnp.maximum, [m for m, _ in stats])
    weights = [jnp.exp2(m - top) for m, _ in stats]
    total = sum(w * l for w, (_, l) in zip(weights, stats))
    if last:
        weights = [w / total for w in weights]
    else:
        out_stats(top, total)
    for h in range(HALF):
        mixed = sum(
            w[..., h : h + 1] * part(h).astype(jnp.float32) for w, part in zip(weights, parts)
        )
        out(h, mixed.astype(jnp.bfloat16))


def kernel(
    q_hbm, kv_hbm, text_hbm, mask_hbm, pat_ref, video_hbm, tout_ref,
    text_ref, mask_ref, video_ref, buf, q, stage, G, T, bias_ref, bias2_ref, Pt, PS, RB1, RS1, P2, S2, RB2, RS2, P3, S3, RB3, RS3, TT, ST, full,
    lsem, g_s, g_r, a_s, a_r, b_s, b_r, x_s, x_r, pair_s, pair_r, hs, hr, fwd_s, r_s, r_r,
):
    t = lax.axis_index("ta")
    s = lax.axis_index("sa")
    core = lax.rem(t, 2)
    y = lax.rem(t // 2, 4)
    x = lax.rem(s, 4)
    z = (t // 8) * 2 + s // 4
    g = x * 2 + core

    def dev(x_, y_, z_, core_):
        return ((z_ // 2) * 8 + y_ * 2 + core_, lax.rem(z_, 2) * 4 + x_)

    def up(v, i, n=4):
        return lax.rem(v + i, n)

    pair_t = t + 1 - 2 * core
    far_t = t + 2 * core - 1
    has_far = jnp.logical_and(far_t >= 0, far_t <= 15)
    has_left = s > 0
    has_right = s < 7
    far_cross = jnp.logical_or(t == 7, t == 8)
    far_relay = jnp.logical_or(t == 0, t == 15)

    def g_peer(i):
        gg = up(g, i, 8)
        return dev(gg // 2, y, z, lax.rem(gg, 2))

    own_copy = pltpu.make_async_copy(kv_hbm, buf.at[OWN], lsem.at[0])
    q_copy = pltpu.make_async_copy(q_hbm, q, lsem.at[1])
    text_copy = pltpu.make_async_copy(text_hbm, text_ref, lsem.at[2])
    mask_copy = pltpu.make_async_copy(mask_hbm, mask_ref, lsem.at[3])
    text_copy.start()
    mask_copy.start()
    barrier = pltpu.get_barrier_semaphore()

    def greet(device):
        pl.semaphore_signal(barrier, inc=1, device_id=device, device_id_type=MESH)

    for i in range(1, 8):
        greet(g_peer(i))
    for i in range(1, 4):
        greet(dev(x, y, up(z, i), core))
        greet(dev(x, up(y, i), z, core))
    extra = [
        (has_far, (far_t, s)),
        (t == 15, (8, s)),
        (t == 8, (15, s)),
        (t == 0, (7, s)),
        (t == 7, (0, s)),
    ]
    for cond, device in extra:

        @pl.when(cond)
        def _():
            greet(device)

    own_copy.start()
    q_copy.start()
    text_copy.wait()
    rows = text_ref[...].astype(jnp.float32)
    w8 = TCOLS // 8
    stage[...] = jnp.concatenate(
        [rows[:, j * w8 : (j + 1) * w8] for j in range(8)], axis=0
    ).astype(jnp.bfloat16)

    pl.semaphore_wait(barrier, 13 + sum(jnp.where(cond, 1, 0) for cond, _ in extra))

    def remote(src, dst, ssem, rsem, device):
        return pltpu.make_async_remote_copy(
            src_ref=src, dst_ref=dst, send_sem=ssem, recv_sem=rsem,
            device_id=device, device_id_type=MESH,
        )

    def g_copy(i, slot):
        return remote(stage, G.at[slot], g_s.at[i], g_r.at[i], g_peer(i))

    for i in range(1, 8):
        g_copy(i, g).start()
    G[pl.ds(g, 1)] = stage[...][None]

    def cols(c, sec):
        return pl.ds(pl.multiple_of(c * CW + sec * D, 128), CW)

    def halo(k, c, sec, src, slot, device):
        return remote(
            src.at[:, cols(c, sec)], buf.at[slot, :, cols(c, sec)],
            hs.at[k], hr.at[slot, c, sec], device,
        )

    def send_halo(k, c):
        odd = lax.rem(c, 2) == 1
        if k == FAR:
            out_t = jnp.where((t == 7) == odd, 15, 0)
            device = (jnp.where(far_cross, out_t, far_t), s)
            slot = FAR
        else:
            edge = 3 if k == RIGHT else 4
            out_s = jnp.where((s == 3) == odd, 7, 0)
            normal = s + 1 if k == RIGHT else s - 1
            device = (t, jnp.where(s == edge, out_s, normal))
            slot = jnp.where(s == edge, jnp.where(out_s == 7, RIGHT, LEFT), LEFT if k == RIGHT else RIGHT)
        for sec in range(2):
            halo(k, c, sec, kv_hbm, slot, device).start()

    def send_loop(first, last, conds, stride=1):
        @functools.partial(lax.fori_loop, 0, (last - first + stride - 1) // stride, init_val=0)
        def _(n, carry):
            c = first + n * stride
            for k, cond in conds:

                @pl.when(cond)
                def _():
                    send_halo(k, c)

            return carry

    along_x = [
        (LEFT, jnp.logical_and(has_left, s != 4)),
        (RIGHT, jnp.logical_and(has_right, s != 3)),
    ]
    crossing = [(LEFT, s == 4), (RIGHT, s == 3)]
    send_loop(0, 1, along_x + crossing)
    send_loop(0, FAR_EARLY, [(FAR, has_far)])
    send_loop(1, 2, crossing)
    send_loop(1, X_EARLY, along_x)
    send_loop(2, CHUNKS, crossing, 2)

    def pair_copy():
        return remote(kv_hbm, buf.at[PAIR], pair_s, pair_r, (pair_t, s))

    pair_copy().start()

    def forward(cond, c, sem, slot, to_slot, device):
        @pl.when(cond)
        def _():
            for sec in range(2):
                halo(0, c, sec, kv_hbm, slot, device).wait_recv()
                remote(
                    buf.at[slot, :, cols(c, sec)], buf.at[to_slot, :, cols(c, sec)],
                    sem, hr.at[to_slot, c, sec], device,
                ).start()

    def relay_x(c, on=True):
        odd = lax.rem(c, 2) == 1
        to_s = jnp.where((s == 7) == odd, 4, 3)
        edge = jnp.logical_and(jnp.logical_or(s == 0, s == 7), on)
        slot = jnp.where(s == 7, RIGHT, LEFT)
        forward(edge, c, fwd_s.at[0], slot, jnp.where(to_s == 4, LEFT, RIGHT), (t, to_s))

    def relay_t(c, on=True):
        odd = lax.rem(c, 2) == 1
        to_t = jnp.where((t == 15) == odd, 8, 7)
        forward(jnp.logical_and(far_relay, on), c, fwd_s.at[1], FAR, FAR, (to_t, s))

    for i in range(1, 8):
        g_copy(i, up(g, 8 - i, 8)).wait_recv()
    r_ = lax.broadcasted_iota(jnp.int32, (128, 128), 0)
    c_ = lax.broadcasted_iota(jnp.int32, (128, 128), 1)
    swap = (r_ // 16 == lax.rem(c_, 16) // 2) & (lax.rem(r_, 16) // 2 == c_ // 16)
    swap = swap & (lax.rem(r_, 2) == lax.rem(c_, 2))
    mixed_rows = jnp.dot(
        jnp.where(swap, 1.0, 0.0).astype(jnp.bfloat16),
        G[...].reshape(128, w8),
        preferred_element_type=jnp.float32,
    ).astype(jnp.bfloat16)
    def place(cc):
        for sec in range(3):
            for n in range(4):
                p = (sec * 4 + cc * 2) * 2 + n
                j, off = p // 3, (p % 3) * 384
                col = cc * THALF + (n // 2) * TQ + sec * SEC + (n % 2) * 384
                T[pl.ds(y, 1), pl.ds(z, 1), :, col : col + 384] = mixed_rows[
                    16 * j : 16 * j + 16, off : off + 384
                ][None, None]

    pl.when(core == 0)(lambda: place(0))
    pl.when(core == 1)(lambda: place(1))

    base = core * THALF

    def step_copy(step, part, half, i, yy, zz):
        along_z = (step == 0) == (half == 0)
        width = (TQ, SEC, 2 * SEC)[part]
        cs = pl.ds(pl.multiple_of(base + half * TQ + (SEC if part == 2 else 0), 128), width)
        if step == 0:
            ref = T.at[yy, zz, :, cs]
        elif half == 0:
            ref = T.at[yy, :, :, cs]
        else:
            ref = T.at[:, zz, :, cs]
        device = dev(x, y, up(z, i), core) if along_z else dev(x, up(y, i), z, core)
        return remote(ref, ref, a_s.at[part, half, i], a_r.at[part, half, i], device)

    def step_starts(step, part):
        for i in (2, 1, 3):
            for half in range(2):
                step_copy(step, part, half, i, y, z).start()

    def step_waits(step, part):
        for half in range(2):
            along_z = (step == 0) == (half == 0)
            for i in range(1, 4):
                if along_z:
                    step_copy(step, part, half, i, y, up(z, 4 - i)).wait_recv()
                else:
                    step_copy(step, part, half, i, up(y, 4 - i), z).wait_recv()

    step_starts(0, 0)
    relay_x(0)
    relay_t(0)
    step_waits(0, 0)
    step_starts(1, 1)
    step_starts(1, 2)
    send_loop(3, 6, crossing, 2)
    send_loop(3, CHUNKS, [(FAR, far_cross)], 2)

    r_ = lax.broadcasted_iota(jnp.int32, (256, 256), 0)
    c_ = lax.broadcasted_iota(jnp.int32, (256, 256), 1)
    by, bz, bx = c_ // 64, lax.rem(c_ // 16, 4), lax.rem(c_, 16) // 4
    bc, bi = lax.rem(c_ // 2, 2), lax.rem(c_, 2)
    row_of = (((bz // 2) * 8 + by * 2 + bc) * 8 + lax.rem(bz, 2) * 4 + bx) * 2 + bi
    mask_copy.wait()
    valid = jnp.where(mask_ref[...] == 1, 1.0, 0.0)
    hot = jnp.where(r_ == row_of, 1.0, 0.0).astype(jnp.bfloat16)
    kept = jnp.dot(
        jnp.broadcast_to(valid, (8, 256)).astype(jnp.bfloat16), hot,
        preferred_element_type=jnp.float32,
    )
    bias = jnp.where(kept > 0.5, 0.0, NEG)
    bias_ref[...] = bias
    lane = lax.broadcasted_iota(jnp.int32, (8, 256), 1)
    bias2_ref[...] = jnp.where(lane // 64 == x, bias, NEG)

    own_copy.wait()
    q_copy.wait()
    pair_copy().wait_recv()
    step_waits(1, 1)
    for c in (2, 4):
        relay_x(c)
    relay_t(2)
    PS[...] = jnp.zeros_like(PS)

    def hcol(v):
        return pl.ds(pl.multiple_of(v, 128), HEAD)

    def text_cols(col):
        return T[:, :, :, hcol(col)].reshape(256, HEAD)

    @functools.partial(lax.fori_loop, 0, HALF, init_val=0)
    def _(hh, carry):
        col = base + (hh // 6) * TQ + lax.rem(hh, 6) * HEAD
        kcol = core * (D // 2) + hh * HEAD
        qx = text_cols(col)
        parts = [
            (qk(qx, buf[OWN, :, hcol(kcol)]), buf[OWN, :, hcol(kcol + D)]),
            (qk(qx, buf[PAIR, :, hcol(kcol)]), buf[PAIR, :, hcol(kcol + D)]),
        ]
        top = functools.reduce(
            jnp.maximum, [jnp.max(sc, axis=1, keepdims=True) for sc, _ in parts]
        ) * C2
        ws = [jnp.exp2(sc * C2 - top) for sc, _ in parts]
        total = sum(jnp.sum(w, axis=1, keepdims=True) for w in ws)
        mixed = sum(pv(w, v) for w, (_, v) in zip(ws, parts))
        Pt[:, :, :, hcol(hh * HEAD)] = mixed.astype(jnp.bfloat16).reshape(4, 4, 16, HEAD)
        here = lax.broadcasted_iota(jnp.int32, (256, HEAD), 1) == hh
        for n, v in ((0, top), (1, total)):
            old = PS[n].reshape(256, HEAD)
            PS[n] = jnp.where(here, v, old).reshape(4, 4, 16, HEAD)
        return carry

    def r1(i, yy):
        device = dev(x, up(y, i), z, core)
        return (
            remote(Pt.at[yy], RB1.at[i - 1], r_s.at[0, i], r_r.at[0, i], device),
            remote(PS.at[:, yy], RS1.at[i - 1], r_s.at[1, i], r_r.at[1, i], device),
        )

    def r2(i, zz):
        device = dev(x, y, up(z, i), core)
        return (
            remote(P2.at[zz], RB2.at[i - 1], r_s.at[2, i], r_r.at[2, i], device),
            remote(S2.at[:, zz], RS2.at[i - 1], r_s.at[3, i], r_r.at[3, i], device),
        )

    def r3(i):
        device = dev(up(x, i), y, z, core)
        return (
            remote(P3, RB3.at[i - 1], r_s.at[4, i], r_r.at[4, i], device),
            remote(S3, RS3.at[i - 1], r_s.at[5, i], r_r.at[5, i], device),
        )

    for i in range(1, 4):
        for cp in r1(i, up(y, i)):
            cp.start()
    send_loop(FAR_EARLY, CHUNKS, [(FAR, jnp.logical_and(has_far, jnp.logical_not(far_cross)))])
    send_loop(4, CHUNKS, [(FAR, far_cross)], 2)

    step_waits(1, 2)

    def half_copy(ab, which):
        cs = pl.ds(pl.multiple_of(which * THALF + ab * TQ + SEC, 128), 2 * SEC)
        ref = T.at[:, :, :, cs]
        return remote(ref, ref, b_s.at[ab], b_r.at[ab], (pair_t, s))

    for ab in range(2):
        half_copy(ab, core).start()

    ST[...] = jnp.zeros_like(ST)

    @functools.partial(lax.fori_loop, 0, HALF, init_val=0)
    def _(hh, carry):
        col = base + (hh // 6) * TQ + lax.rem(hh, 6) * HEAD
        sc = qk(T[y, z, :, hcol(col)], text_cols(col + SEC)) + bias2_ref[0:1, :]
        top = jnp.max(sc, axis=1, keepdims=True) * C2
        w = jnp.exp2(sc * C2 - top)
        TT[:, hcol(hh * HEAD)] = pv(w, text_cols(col + 2 * SEC)).astype(jnp.bfloat16)
        here = lax.broadcasted_iota(jnp.int32, (16, HEAD), 1) == hh
        for n, v in ((0, top), (1, jnp.sum(w, axis=1, keepdims=True))):
            ST[n] = jnp.where(here, v, ST[n])
        return carry


    def merge1():
        for i in range(1, 4):
            for cp in r1(i, up(y, i)):
                cp.wait_recv()
        stats = [(PS[0, y].reshape(64, HEAD), PS[1, y].reshape(64, HEAD))]
        stats += [(RS1[i, 0].reshape(64, HEAD), RS1[i, 1].reshape(64, HEAD)) for i in range(3)]

        def own(h):
            return Pt[y, :, :, h * HEAD : (h + 1) * HEAD].reshape(64, HEAD)

        def got(i):
            return lambda h: RB1[i, :, :, h * HEAD : (h + 1) * HEAD].reshape(64, HEAD)

        def out(h, v):
            P2[:, :, h * HEAD : (h + 1) * HEAD] = v.reshape(4, 16, HEAD)

        def out_stats(m, l):
            S2[0] = m.reshape(4, 16, HEAD)
            S2[1] = l.reshape(4, 16, HEAD)

        merge([own] + [got(i) for i in range(3)], stats, out, out_stats, False)
        for i in range(1, 4):
            for cp in r2(i, up(z, i)):
                cp.start()

    def merge2():
        for i in range(1, 4):
            for cp in r2(i, up(z, i)):
                cp.wait_recv()
        stats = [(S2[0, z], S2[1, z])] + [(RS2[i, 0], RS2[i, 1]) for i in range(3)]
        stats.append((ST[0], ST[1]))

        def local_text(h):
            return TT[:, h * HEAD : (h + 1) * HEAD]

        def own(h):
            return P2[z, :, h * HEAD : (h + 1) * HEAD]

        def got(i):
            return lambda h: RB2[i, :, h * HEAD : (h + 1) * HEAD]

        def out(h, v):
            P3[:, h * HEAD : (h + 1) * HEAD] = v

        def out_stats(m, l):
            S3[0] = m
            S3[1] = l

        merge([own] + [got(i) for i in range(3)] + [local_text], stats, out, out_stats, False)
        for i in range(1, 4):
            for cp in r3(i):
                cp.start()
        send_loop(X_EARLY, CHUNKS, along_x)

    fcols = pl.ds(pl.multiple_of(core * (D // 2), 128), D // 2)
    ocols = pl.ds(pl.multiple_of((1 - core) * (D // 2), 128), D // 2)
    f_out = remote(full.at[:, fcols], full.at[:, fcols], r_s.at[6, 0], r_r.at[6, 0], (pair_t, s))
    f_in = remote(full.at[:, ocols], full.at[:, ocols], r_s.at[6, 0], r_r.at[6, 0], (pair_t, s))

    def merge3():
        for i in range(1, 4):
            for cp in r3(i):
                cp.wait_recv()
        stats = [(S3[0], S3[1])] + [(RS3[i, 0], RS3[i, 1]) for i in range(3)]

        def own(h):
            return P3[:, h * HEAD : (h + 1) * HEAD]

        def got(i):
            return lambda h: RB3[i, :, h * HEAD : (h + 1) * HEAD]

        def out(h, v):
            full[:, hcol(core * (D // 2) + h * HEAD)] = v

        merge([own] + [got(i) for i in range(3)], stats, out, None, True)
        f_out.start()

    for ab in range(2):
        half_copy(ab, 1 - core).wait_recv()
    number = [(pair_t, s), (far_t, s), (t, s - 1), (t, s + 1)]
    exists = [None, has_far, has_left, has_right]
    seen = []
    for k in range(4):
        tile = number[k][0] * 8 + number[k][1]
        hit = jnp.int32(0)
        for n in range(4):
            hit = hit + jnp.where(pat_ref[n] == tile, 1, 0)
        if exists[k] is not None:
            hit = hit * jnp.where(exists[k], 1, 0)
        seen.append(hit)
    slots = [PAIR] + [jnp.where(exists[k], k, OWN) for k in (FAR, LEFT, RIGHT)]
    drop = [jnp.where(h > 0, 0.0, NEG).astype(jnp.float32) for h in seen]

    def video(c):
        for k in (FAR, LEFT, RIGHT):

            @pl.when(exists[k])
            def _():
                for sec in range(2):
                    halo(0, c, sec, kv_hbm, k, (t, s)).wait_recv()

        for hh in range(2):
            col = c * CW + hh * HEAD
            tcol = (c // 3) * TQ + lax.rem(c, 3) * CW + hh * HEAD
            qh = q[:, hcol(col)]
            sc = [qk(qh, buf[OWN, :, hcol(col)])]
            sc += [qk(qh, buf[slots[k], :, hcol(col)]) for k in range(4)]
            sc.append(qk(qh, text_cols(tcol + SEC)) + bias_ref[0:1, :])
            tops = [jnp.max(v, axis=1, keepdims=True) for v in sc]
            for k in range(4):
                tops[1 + k] = tops[1 + k] + drop[k]
            top = functools.reduce(jnp.maximum, tops) * C2
            lows = [top] + [top - drop[k] for k in range(4)] + [top]
            ws = [jnp.exp2(v * C2 - low) for v, low in zip(sc, lows)]
            total = sum(jnp.sum(w, axis=1, keepdims=True) for w in ws)
            vs = [buf[OWN, :, hcol(col + D)]]
            vs += [buf[slots[k], :, hcol(col + D)] for k in range(4)]
            vs.append(text_cols(tcol + 2 * SEC))
            mixed = sum(pv(w, v) for w, v in zip(ws, vs))
            video_ref[:, hcol(col)] = (mixed / total).astype(jnp.bfloat16)
        span = pl.ds(pl.multiple_of(c * CW, 128), CW)
        pltpu.make_async_copy(video_ref.at[:, span], video_hbm.at[:, span], lsem.at[4]).start()

    relay_x(1)
    relay_t(1)

    @functools.partial(lax.fori_loop, 0, CHUNKS, init_val=0)
    def _(c, carry):
        pl.when(c == AT1)(merge1)
        relay_t(3, c == AT1)
        relay_x(jnp.where(c == AT1, 6, c + 6), jnp.logical_or(c == AT1, jnp.logical_and(lax.rem(c, 2) == 0, jnp.logical_and(c > 0, c < 6))))

        @pl.when(jnp.logical_or(c == AT1, jnp.logical_and(lax.rem(c, 2) == 0, jnp.logical_and(c > 0, c < 6))))
        def _():
            for k, cond in crossing:

                @pl.when(cond)
                def _():
                    send_halo(k, jnp.where(c == AT1, 7, c + 7))

        relay_x(c + 2, jnp.logical_and(lax.rem(c, 2) == 1, c < 10))
        relay_t(c + 3, jnp.logical_and(c >= AT1, c < CHUNKS - 3))
        pl.when(c == AT2)(merge2)
        pl.when(c == CHUNKS - 1)(merge3)
        video(c)
        return carry

    f_in.wait_recv()
    pick_r = lax.broadcasted_iota(jnp.int32, (16, 16), 0)
    pick_c = lax.broadcasted_iota(jnp.int32, (16, 16), 1)
    pick = jnp.where(pick_c == pick_r + 2 * g, 1.0, 0.0).astype(jnp.bfloat16)
    chosen = jnp.dot(pick, full[...], preferred_element_type=jnp.float32)
    tout_ref[...] = chosen[:2].astype(jnp.bfloat16)

    pltpu.make_async_copy(video_ref, video_hbm, lsem.at[4]).wait()
    for i in range(1, 8):
        g_copy(i, g).wait_send()
    for part in range(3):
        for i in range(1, 4):
            for half in range(2):
                step_copy(min(part, 1), part, half, i, y, z).wait_send()
    for ab in range(2):
        half_copy(ab, core).wait_send()
    pair_copy().wait_send()

    def drain(cond, sem, width):
        @pl.when(cond)
        def _():
            ref = buf.at[OWN, :, pl.ds(0, width)]
            remote(ref, ref, sem, hr.at[0, 0, 0], (pair_t, s)).wait_send()

    drain(has_far, hs.at[FAR], 2 * D)
    drain(has_left, hs.at[LEFT], 2 * D)
    drain(has_right, hs.at[RIGHT], 2 * D)
    drain(jnp.logical_or(s == 0, s == 7), fwd_s.at[0], 2 * D)
    drain(far_relay, fwd_s.at[1], 2 * D)
    for i in range(1, 4):
        for cp in r1(i, up(y, i)) + r2(i, up(z, i)) + r3(i):
            cp.wait_send()
    f_out.wait_send()


def local(video_q, video_kv, text_qkv, text_mask, pattern):
    bf, f32 = jnp.bfloat16, jnp.float32
    dma = pltpu.SemaphoreType.DMA
    vm = pltpu.VMEM
    whole = pl.BlockSpec(memory_space=pltpu.VMEM)
    hbm = pl.BlockSpec(memory_space=pl.ANY)
    scratch = [
        vm((2, TCOLS), bf),
        vm((1, 256), jnp.int32),
        vm((TILE, D), bf),
        vm((5, TILE, 2 * D), bf),
        vm((TILE, D), bf),
        vm((16, TCOLS // 8), bf),
        vm((8, 16, TCOLS // 8), bf),
        vm((4, 4, 16, TCOLS), bf),
        vm((8, 256), f32),
        vm((8, 256), f32),
        vm((4, 4, 16, D // 2), bf),
        vm((2, 4, 4, 16, HEAD), f32),
        vm((3, 4, 16, D // 2), bf),
        vm((3, 2, 4, 16, HEAD), f32),
        vm((4, 16, D // 2), bf),
        vm((2, 4, 16, HEAD), f32),
        vm((3, 16, D // 2), bf),
        vm((3, 2, 16, HEAD), f32),
        vm((16, D // 2), bf),
        vm((2, 16, HEAD), f32),
        vm((3, 16, D // 2), bf),
        vm((3, 2, 16, HEAD), f32),
        vm((16, D // 2), bf),
        vm((2, 16, HEAD), f32),
        vm((16, D), bf),
        dma((5,)), dma((8,)), dma((8,)), dma((3, 2, 4)), dma((3, 2, 4)),
        dma((2,)), dma((2,)), dma, dma, dma, dma, dma((4,)), dma((4, CHUNKS, 2)), dma((2,)), dma((7, 4)), dma((7, 4)),
    ]
    video_out, text_out = pl.pallas_call(
        kernel,
        out_shape=(jax.ShapeDtypeStruct((TILE, D), bf), jax.ShapeDtypeStruct((2, D), bf)),
        in_specs=[hbm, hbm, hbm, hbm, pl.BlockSpec(memory_space=pltpu.SMEM)],
        out_specs=(hbm, whole),
        scratch_shapes=scratch,
        compiler_params=pltpu.CompilerParams(
            collective_id=0, has_side_effects=True, vmem_limit_bytes=58 * 2**20
        ),
        cost_estimate=pl.CostEstimate(
            flops=6 * 10**9, bytes_accessed=10**7, transcendentals=12 * 10**6
        ),
    )(video_q[0, 0], video_kv[0, 0], text_qkv, text_mask.reshape(1, 256), pattern.reshape(4))
    return video_out[None, None], text_out


def solution(mesh):
    in_specs = (
        P("ta", "sa", None, None),
        P("ta", "sa", None, None),
        P(("ta", "sa"), None),
        P(),
        P("ta", "sa", None),
    )
    out_specs = (P("ta", "sa", None, None), P(("ta", "sa"), None))
    return jax.shard_map(local, mesh=mesh, in_specs=in_specs, out_specs=out_specs, check_vma=False)
```

```python
import functools
import math

import jax
import jax.numpy as jnp
from jax import lax
from jax.experimental import pallas as pl
from jax.experimental.pallas import tpu as pltpu
from jax.sharding import PartitionSpec as P

HEAD = 128
D = 3072
TILE = 256
HEADS = 24
HALF = 12
CHUNKS = 12
CW = D // CHUNKS
TCOLS = 3 * D
THALF = TCOLS // 2
TQ = THALF // 2
SEC = TQ // 3
MESH = pl.DeviceIdType.MESH
C2 = math.log2(math.e) / math.sqrt(HEAD)
NEG = -1e30
FAR_EARLY, X_EARLY, AT1, AT2 = 3, 11, 1, 6
PAIR, FAR, LEFT, RIGHT, OWN = 0, 1, 2, 3, 4


def qk(q, k):
    return lax.dot_general(q, k, (((1,), (1,)), ((), ())), preferred_element_type=jnp.float32)


def pv(p, v):
    return jnp.dot(p.astype(jnp.bfloat16), v, preferred_element_type=jnp.float32)


def merge(parts, stats, out, out_stats, last):
    top = functools.reduce(jnp.maximum, [m for m, _ in stats])
    weights = [jnp.exp2(m - top) for m, _ in stats]
    total = sum(w * l for w, (_, l) in zip(weights, stats))
    if last:
        weights = [w / total for w in weights]
    else:
        out_stats(top, total)
    for h in range(HALF):
        mixed = sum(
            w[..., h : h + 1] * part(h).astype(jnp.float32) for w, part in zip(weights, parts)
        )
        out(h, mixed.astype(jnp.bfloat16))


def kernel(
    q_hbm, kv_hbm, text_hbm, mask_hbm, pat_ref, video_hbm, tout_ref,
    text_ref, mask_ref, video_ref, buf, q, stage, G, T, bias_ref, bias2_ref, Pt, PS, RB1, RS1, P2, S2, RB2, RS2, P3, S3, RB3, RS3, TT, ST, full,
    lsem, g_s, g_r, a_s, a_r, b_s, b_r, x_s, x_r, pair_s, pair_r, hs, hr, fwd_s, r_s, r_r,
):
    t = lax.axis_index("ta")
    s = lax.axis_index("sa")
    core = lax.rem(t, 2)
    y = lax.rem(t // 2, 4)
    x = lax.rem(s, 4)
    z = (t // 8) * 2 + s // 4
    g = x * 2 + core

    def dev(x_, y_, z_, core_):
        return ((z_ // 2) * 8 + y_ * 2 + core_, lax.rem(z_, 2) * 4 + x_)

    def up(v, i, n=4):
        return lax.rem(v + i, n)

    pair_t = t + 1 - 2 * core
    far_t = t + 2 * core - 1
    has_far = jnp.logical_and(far_t >= 0, far_t <= 15)
    has_left = s > 0
    has_right = s < 7
    far_cross = jnp.logical_or(t == 7, t == 8)
    far_relay = jnp.logical_or(t == 0, t == 15)

    def g_peer(i):
        gg = up(g, i, 8)
        return dev(gg // 2, y, z, lax.rem(gg, 2))

    own_copy = pltpu.make_async_copy(kv_hbm, buf.at[OWN], lsem.at[0])
    q_copy = pltpu.make_async_copy(q_hbm, q, lsem.at[1])
    text_copy = pltpu.make_async_copy(text_hbm, text_ref, lsem.at[2])
    mask_copy = pltpu.make_async_copy(mask_hbm, mask_ref, lsem.at[3])
    text_copy.start()
    mask_copy.start()
    barrier = pltpu.get_barrier_semaphore()

    def greet(device):
        pl.semaphore_signal(barrier, inc=1, device_id=device, device_id_type=MESH)

    for i in range(1, 8):
        greet(g_peer(i))
    for i in range(1, 4):
        greet(dev(x, y, up(z, i), core))
        greet(dev(x, up(y, i), z, core))
    extra = [
        (has_far, (far_t, s)),
        (t == 15, (8, s)),
        (t == 8, (15, s)),
        (t == 0, (7, s)),
        (t == 7, (0, s)),
    ]
    for cond, device in extra:

        @pl.when(cond)
        def _():
            greet(device)

    own_copy.start()
    q_copy.start()
    text_copy.wait()
    rows = text_ref[...].astype(jnp.float32)
    w8 = TCOLS // 8
    stage[...] = jnp.concatenate(
        [rows[:, j * w8 : (j + 1) * w8] for j in range(8)], axis=0
    ).astype(jnp.bfloat16)

    pl.semaphore_wait(barrier, 13 + sum(jnp.where(cond, 1, 0) for cond, _ in extra))

    def remote(src, dst, ssem, rsem, device):
        return pltpu.make_async_remote_copy(
            src_ref=src, dst_ref=dst, send_sem=ssem, recv_sem=rsem,
            device_id=device, device_id_type=MESH,
        )

    def g_copy(i, slot):
        return remote(stage, G.at[slot], g_s.at[i], g_r.at[i], g_peer(i))

    for i in range(1, 8):
        g_copy(i, g).start()
    G[pl.ds(g, 1)] = stage[...][None]

    def cols(c, sec):
        return pl.ds(pl.multiple_of(c * CW + sec * D, 128), CW)

    def halo(k, c, sec, src, slot, device):
        return remote(
            src.at[:, cols(c, sec)], buf.at[slot, :, cols(c, sec)],
            hs.at[k], hr.at[slot, c, sec], device,
        )

    def send_halo(k, c):
        odd = lax.rem(c, 2) == 1
        if k == FAR:
            out_t = jnp.where((t == 7) == odd, 15, 0)
            device = (jnp.where(far_cross, out_t, far_t), s)
            slot = FAR
        else:
            edge = 3 if k == RIGHT else 4
            out_s = jnp.where((s == 3) == odd, 7, 0)
            normal = s + 1 if k == RIGHT else s - 1
            device = (t, jnp.where(s == edge, out_s, normal))
            slot = jnp.where(s == edge, jnp.where(out_s == 7, RIGHT, LEFT), LEFT if k == RIGHT else RIGHT)
        for sec in range(2):
            halo(k, c, sec, kv_hbm, slot, device).start()

    def send_loop(first, last, conds, stride=1):
        @functools.partial(lax.fori_loop, 0, (last - first + stride - 1) // stride, init_val=0)
        def _(n, carry):
            c = first + n * stride
            for k, cond in conds:

                @pl.when(cond)
                def _():
                    send_halo(k, c)

            return carry

    along_x = [
        (LEFT, jnp.logical_and(has_left, s != 4)),
        (RIGHT, jnp.logical_and(has_right, s != 3)),
    ]
    crossing = [(LEFT, s == 4), (RIGHT, s == 3)]
    send_loop(0, 1, along_x + crossing)
    send_loop(0, FAR_EARLY, [(FAR, has_far)])
    send_loop(1, 2, crossing)
    send_loop(4, 5, [(FAR, far_cross)])
    send_loop(1, X_EARLY, along_x)
    send_loop(2, CHUNKS, crossing, 2)

    def pair_copy():
        return remote(kv_hbm, buf.at[PAIR], pair_s, pair_r, (pair_t, s))

    pair_copy().start()

    def forward(cond, c, sem, slot, to_slot, device):
        @pl.when(cond)
        def _():
            for sec in range(2):
                halo(0, c, sec, kv_hbm, slot, device).wait_recv()
                remote(
                    buf.at[slot, :, cols(c, sec)], buf.at[to_slot, :, cols(c, sec)],
                    sem, hr.at[to_slot, c, sec], device,
                ).start()

    def relay_x(c, on=True):
        odd = lax.rem(c, 2) == 1
        to_s = jnp.where((s == 7) == odd, 4, 3)
        edge = jnp.logical_and(jnp.logical_or(s == 0, s == 7), on)
        slot = jnp.where(s == 7, RIGHT, LEFT)
        forward(edge, c, fwd_s.at[0], slot, jnp.where(to_s == 4, LEFT, RIGHT), (t, to_s))

    def relay_t(c, on=True):
        odd = lax.rem(c, 2) == 1
        to_t = jnp.where((t == 15) == odd, 8, 7)
        forward(jnp.logical_and(far_relay, on), c, fwd_s.at[1], FAR, FAR, (to_t, s))

    for i in range(1, 8):
        g_copy(i, up(g, 8 - i, 8)).wait_recv()
    r_ = lax.broadcasted_iota(jnp.int32, (128, 128), 0)
    c_ = lax.broadcasted_iota(jnp.int32, (128, 128), 1)
    swap = (r_ // 16 == lax.rem(c_, 16) // 2) & (lax.rem(r_, 16) // 2 == c_ // 16)
    swap = swap & (lax.rem(r_, 2) == lax.rem(c_, 2))
    mixed_rows = jnp.dot(
        jnp.where(swap, 1.0, 0.0).astype(jnp.bfloat16),
        G[...].reshape(128, w8),
        preferred_element_type=jnp.float32,
    ).astype(jnp.bfloat16)
    def place(cc):
        for sec in range(3):
            for n in range(4):
                p = (sec * 4 + cc * 2) * 2 + n
                j, off = p // 3, (p % 3) * 384
                col = cc * THALF + (n // 2) * TQ + sec * SEC + (n % 2) * 384
                T[pl.ds(y, 1), pl.ds(z, 1), :, col : col + 384] = mixed_rows[
                    16 * j : 16 * j + 16, off : off + 384
                ][None, None]

    pl.when(core == 0)(lambda: place(0))
    pl.when(core == 1)(lambda: place(1))

    base = core * THALF

    def step_copy(step, part, half, i, yy, zz):
        along_z = (step == 0) == (half == 0)
        width = (TQ, SEC, 2 * SEC)[part]
        cs = pl.ds(pl.multiple_of(base + half * TQ + (SEC if part == 2 else 0), 128), width)
        if step == 0:
            ref = T.at[yy, zz, :, cs]
        elif half == 0:
            ref = T.at[yy, :, :, cs]
        else:
            ref = T.at[:, zz, :, cs]
        device = dev(x, y, up(z, i), core) if along_z else dev(x, up(y, i), z, core)
        return remote(ref, ref, a_s.at[part, half, i], a_r.at[part, half, i], device)

    def step_starts(step, part):
        for i in (2, 1, 3):
            for half in range(2):
                step_copy(step, part, half, i, y, z).start()

    def step_waits(step, part):
        for half in range(2):
            along_z = (step == 0) == (half == 0)
            for i in range(1, 4):
                if along_z:
                    step_copy(step, part, half, i, y, up(z, 4 - i)).wait_recv()
                else:
                    step_copy(step, part, half, i, up(y, 4 - i), z).wait_recv()

    step_starts(0, 0)
    relay_x(0)
    relay_t(0)
    step_waits(0, 0)
    step_starts(1, 1)
    step_starts(1, 2)
    send_loop(3, 6, crossing, 2)
    send_loop(3, CHUNKS, [(FAR, far_cross)], 2)

    r_ = lax.broadcasted_iota(jnp.int32, (256, 256), 0)
    c_ = lax.broadcasted_iota(jnp.int32, (256, 256), 1)
    by, bz, bx = c_ // 64, lax.rem(c_ // 16, 4), lax.rem(c_, 16) // 4
    bc, bi = lax.rem(c_ // 2, 2), lax.rem(c_, 2)
    row_of = (((bz // 2) * 8 + by * 2 + bc) * 8 + lax.rem(bz, 2) * 4 + bx) * 2 + bi
    mask_copy.wait()
    valid = jnp.where(mask_ref[...] == 1, 1.0, 0.0)
    hot = jnp.where(r_ == row_of, 1.0, 0.0).astype(jnp.bfloat16)
    kept = jnp.dot(
        jnp.broadcast_to(valid, (8, 256)).astype(jnp.bfloat16), hot,
        preferred_element_type=jnp.float32,
    )
    bias = jnp.where(kept > 0.5, 0.0, NEG)
    bias_ref[...] = bias
    lane = lax.broadcasted_iota(jnp.int32, (8, 256), 1)
    bias2_ref[...] = jnp.where(lane // 64 == x, bias, NEG)

    own_copy.wait()
    q_copy.wait()
    pair_copy().wait_recv()
    step_waits(1, 1)
    for c in (2, 4):
        relay_x(c)
    relay_t(2)
    PS[...] = jnp.zeros_like(PS)

    def hcol(v):
        return pl.ds(pl.multiple_of(v, 128), HEAD)

    def text_cols(col):
        return T[:, :, :, hcol(col)].reshape(256, HEAD)

    @functools.partial(lax.fori_loop, 0, HALF, init_val=0, unroll=2)
    def _(hh, carry):
        col = base + (hh // 6) * TQ + lax.rem(hh, 6) * HEAD
        kcol = core * (D // 2) + hh * HEAD
        qx = text_cols(col)
        parts = [
            (qk(qx, buf[OWN, :, hcol(kcol)]), buf[OWN, :, hcol(kcol + D)]),
            (qk(qx, buf[PAIR, :, hcol(kcol)]), buf[PAIR, :, hcol(kcol + D)]),
        ]
        top = functools.reduce(
            jnp.maximum, [jnp.max(sc, axis=1, keepdims=True) for sc, _ in parts]
        ) * C2
        ws = [jnp.exp2(sc * C2 - top) for sc, _ in parts]
        total = sum(jnp.sum(w, axis=1, keepdims=True) for w in ws)
        mixed = sum(pv(w, v) for w, (_, v) in zip(ws, parts))
        Pt[:, :, :, hcol(hh * HEAD)] = mixed.astype(jnp.bfloat16).reshape(4, 4, 16, HEAD)
        here = lax.broadcasted_iota(jnp.int32, (256, HEAD), 1) == hh
        for n, v in ((0, top), (1, total)):
            old = PS[n].reshape(256, HEAD)
            PS[n] = jnp.where(here, v, old).reshape(4, 4, 16, HEAD)
        return carry

    def r1(i, yy):
        device = dev(x, up(y, i), z, core)
        return (
            remote(Pt.at[yy], RB1.at[i - 1], r_s.at[0, i], r_r.at[0, i], device),
            remote(PS.at[:, yy], RS1.at[i - 1], r_s.at[1, i], r_r.at[1, i], device),
        )

    def r2(i, zz):
        device = dev(x, y, up(z, i), core)
        return (
            remote(P2.at[zz], RB2.at[i - 1], r_s.at[2, i], r_r.at[2, i], device),
            remote(S2.at[:, zz], RS2.at[i - 1], r_s.at[3, i], r_r.at[3, i], device),
        )

    def r3(i):
        device = dev(up(x, i), y, z, core)
        return (
            remote(P3, RB3.at[i - 1], r_s.at[4, i], r_r.at[4, i], device),
            remote(S3, RS3.at[i - 1], r_s.at[5, i], r_r.at[5, i], device),
        )

    for i in range(1, 4):
        for cp in r1(i, up(y, i)):
            cp.start()
    send_loop(FAR_EARLY, CHUNKS, [(FAR, jnp.logical_and(has_far, jnp.logical_not(far_cross)))])
    send_loop(6, CHUNKS, [(FAR, far_cross)], 2)

    step_waits(1, 2)

    def half_copy(ab, which):
        cs = pl.ds(pl.multiple_of(which * THALF + ab * TQ + SEC, 128), 2 * SEC)
        ref = T.at[:, :, :, cs]
        return remote(ref, ref, b_s.at[ab], b_r.at[ab], (pair_t, s))

    for ab in range(2):
        half_copy(ab, core).start()

    ST[...] = jnp.zeros_like(ST)

    @functools.partial(lax.fori_loop, 0, HALF, init_val=0, unroll=4)
    def _(hh, carry):
        col = base + (hh // 6) * TQ + lax.rem(hh, 6) * HEAD
        sc = qk(T[y, z, :, hcol(col)], text_cols(col + SEC)) + bias2_ref[0:1, :]
        top = jnp.max(sc, axis=1, keepdims=True) * C2
        w = jnp.exp2(sc * C2 - top)
        TT[:, hcol(hh * HEAD)] = pv(w, text_cols(col + 2 * SEC)).astype(jnp.bfloat16)
        here = lax.broadcasted_iota(jnp.int32, (16, HEAD), 1) == hh
        for n, v in ((0, top), (1, jnp.sum(w, axis=1, keepdims=True))):
            ST[n] = jnp.where(here, v, ST[n])
        return carry


    def merge1():
        for i in range(1, 4):
            for cp in r1(i, up(y, i)):
                cp.wait_recv()
        stats = [(PS[0, y].reshape(64, HEAD), PS[1, y].reshape(64, HEAD))]
        stats += [(RS1[i, 0].reshape(64, HEAD), RS1[i, 1].reshape(64, HEAD)) for i in range(3)]

        def own(h):
            return Pt[y, :, :, h * HEAD : (h + 1) * HEAD].reshape(64, HEAD)

        def got(i):
            return lambda h: RB1[i, :, :, h * HEAD : (h + 1) * HEAD].reshape(64, HEAD)

        def out(h, v):
            P2[:, :, h * HEAD : (h + 1) * HEAD] = v.reshape(4, 16, HEAD)

        def out_stats(m, l):
            S2[0] = m.reshape(4, 16, HEAD)
            S2[1] = l.reshape(4, 16, HEAD)

        merge([own] + [got(i) for i in range(3)], stats, out, out_stats, False)
        for i in range(1, 4):
            for cp in r2(i, up(z, i)):
                cp.start()

    def merge2():
        for i in range(1, 4):
            for cp in r2(i, up(z, i)):
                cp.wait_recv()
        stats = [(S2[0, z], S2[1, z])] + [(RS2[i, 0], RS2[i, 1]) for i in range(3)]
        stats.append((ST[0], ST[1]))

        def local_text(h):
            return TT[:, h * HEAD : (h + 1) * HEAD]

        def own(h):
            return P2[z, :, h * HEAD : (h + 1) * HEAD]

        def got(i):
            return lambda h: RB2[i, :, h * HEAD : (h + 1) * HEAD]

        def out(h, v):
            P3[:, h * HEAD : (h + 1) * HEAD] = v

        def out_stats(m, l):
            S3[0] = m
            S3[1] = l

        merge([own] + [got(i) for i in range(3)] + [local_text], stats, out, out_stats, False)
        for i in range(1, 4):
            for cp in r3(i):
                cp.start()
        send_loop(X_EARLY, CHUNKS, along_x)

    fcols = pl.ds(pl.multiple_of(core * (D // 2), 128), D // 2)
    ocols = pl.ds(pl.multiple_of((1 - core) * (D // 2), 128), D // 2)
    f_out = remote(full.at[:, fcols], full.at[:, fcols], r_s.at[6, 0], r_r.at[6, 0], (pair_t, s))
    f_in = remote(full.at[:, ocols], full.at[:, ocols], r_s.at[6, 0], r_r.at[6, 0], (pair_t, s))

    def merge3():
        for i in range(1, 4):
            for cp in r3(i):
                cp.wait_recv()
        stats = [(S3[0], S3[1])] + [(RS3[i, 0], RS3[i, 1]) for i in range(3)]

        def own(h):
            return P3[:, h * HEAD : (h + 1) * HEAD]

        def got(i):
            return lambda h: RB3[i, :, h * HEAD : (h + 1) * HEAD]

        def out(h, v):
            full[:, hcol(core * (D // 2) + h * HEAD)] = v

        merge([own] + [got(i) for i in range(3)], stats, out, None, True)
        f_out.start()

    for ab in range(2):
        half_copy(ab, 1 - core).wait_recv()
    number = [(pair_t, s), (far_t, s), (t, s - 1), (t, s + 1)]
    exists = [None, has_far, has_left, has_right]
    seen = []
    for k in range(4):
        tile = number[k][0] * 8 + number[k][1]
        hit = jnp.int32(0)
        for n in range(4):
            hit = hit + jnp.where(pat_ref[n] == tile, 1, 0)
        if exists[k] is not None:
            hit = hit * jnp.where(exists[k], 1, 0)
        seen.append(hit)
    slots = [PAIR] + [jnp.where(exists[k], k, OWN) for k in (FAR, LEFT, RIGHT)]
    drop = [jnp.where(h > 0, 0.0, NEG).astype(jnp.float32) for h in seen]

    def video(c):
        for k in (FAR, LEFT, RIGHT):

            @pl.when(exists[k])
            def _():
                for sec in range(2):
                    halo(0, c, sec, kv_hbm, k, (t, s)).wait_recv()

        for hh in range(2):
            col = c * CW + hh * HEAD
            tcol = (c // 3) * TQ + lax.rem(c, 3) * CW + hh * HEAD
            qh = q[:, hcol(col)]
            sc = [qk(qh, buf[OWN, :, hcol(col)])]
            sc += [qk(qh, buf[slots[k], :, hcol(col)]) for k in range(4)]
            sc.append(qk(qh, text_cols(tcol + SEC)) + bias_ref[0:1, :])
            tops = [jnp.max(v, axis=1, keepdims=True) for v in sc]
            for k in range(4):
                tops[1 + k] = tops[1 + k] + drop[k]
            top = functools.reduce(jnp.maximum, tops) * C2
            lows = [top] + [top - drop[k] for k in range(4)] + [top]
            ws = [jnp.exp2(v * C2 - low) for v, low in zip(sc, lows)]
            total = sum(jnp.sum(w, axis=1, keepdims=True) for w in ws)
            vs = [buf[OWN, :, hcol(col + D)]]
            vs += [buf[slots[k], :, hcol(col + D)] for k in range(4)]
            vs.append(text_cols(tcol + 2 * SEC))
            mixed = sum(pv(w, v) for w, v in zip(ws, vs))
            video_ref[:, hcol(col)] = (mixed / total).astype(jnp.bfloat16)
        span = pl.ds(pl.multiple_of(c * CW, 128), CW)
        pltpu.make_async_copy(video_ref.at[:, span], video_hbm.at[:, span], lsem.at[4]).start()

    relay_x(1)
    relay_t(1)

    @functools.partial(lax.fori_loop, 0, CHUNKS, init_val=0)
    def _(c, carry):
        pl.when(c == AT1)(merge1)
        relay_t(3, c == AT1)
        relay_x(jnp.where(c == AT1, 6, c + 6), jnp.logical_or(c == AT1, jnp.logical_and(lax.rem(c, 2) == 0, jnp.logical_and(c > 0, c < 6))))

        @pl.when(jnp.logical_or(c == AT1, jnp.logical_and(lax.rem(c, 2) == 0, jnp.logical_and(c > 0, c < 6))))
        def _():
            for k, cond in crossing:

                @pl.when(cond)
                def _():
                    send_halo(k, jnp.where(c == AT1, 7, c + 7))

        relay_x(c + 2, jnp.logical_and(lax.rem(c, 2) == 1, c < 10))
        relay_t(c + 3, jnp.logical_and(c >= AT1, c < CHUNKS - 3))
        pl.when(c == AT2)(merge2)
        pl.when(c == CHUNKS - 1)(merge3)
        video(c)
        return carry

    f_in.wait_recv()
    pick_r = lax.broadcasted_iota(jnp.int32, (16, 16), 0)
    pick_c = lax.broadcasted_iota(jnp.int32, (16, 16), 1)
    pick = jnp.where(pick_c == pick_r + 2 * g, 1.0, 0.0).astype(jnp.bfloat16)
    chosen = jnp.dot(pick, full[...], preferred_element_type=jnp.float32)
    tout_ref[...] = chosen[:2].astype(jnp.bfloat16)

    pltpu.make_async_copy(video_ref, video_hbm, lsem.at[4]).wait()
    for i in range(1, 8):
        g_copy(i, g).wait_send()
    for part in range(3):
        for i in range(1, 4):
            for half in range(2):
                step_copy(min(part, 1), part, half, i, y, z).wait_send()
    for ab in range(2):
        half_copy(ab, core).wait_send()
    pair_copy().wait_send()

    def drain(cond, sem, width):
        @pl.when(cond)
        def _():
            ref = buf.at[OWN, :, pl.ds(0, width)]
            remote(ref, ref, sem, hr.at[0, 0, 0], (pair_t, s)).wait_send()

    drain(has_far, hs.at[FAR], 2 * D)
    drain(has_left, hs.at[LEFT], 2 * D)
    drain(has_right, hs.at[RIGHT], 2 * D)
    drain(jnp.logical_or(s == 0, s == 7), fwd_s.at[0], 2 * D)
    drain(far_relay, fwd_s.at[1], 2 * D)
    for i in range(1, 4):
        for cp in r1(i, up(y, i)) + r2(i, up(z, i)) + r3(i):
            cp.wait_send()
    f_out.wait_send()


def local(video_q, video_kv, text_qkv, text_mask, pattern):
    bf, f32 = jnp.bfloat16, jnp.float32
    dma = pltpu.SemaphoreType.DMA
    vm = pltpu.VMEM
    whole = pl.BlockSpec(memory_space=pltpu.VMEM)
    hbm = pl.BlockSpec(memory_space=pl.ANY)
    scratch = [
        vm((2, TCOLS), bf),
        vm((1, 256), jnp.int32),
        vm((TILE, D), bf),
        vm((5, TILE, 2 * D), bf),
        vm((TILE, D), bf),
        vm((16, TCOLS // 8), bf),
        vm((8, 16, TCOLS // 8), bf),
        vm((4, 4, 16, TCOLS), bf),
        vm((8, 256), f32),
        vm((8, 256), f32),
        vm((4, 4, 16, D // 2), bf),
        vm((2, 4, 4, 16, HEAD), f32),
        vm((3, 4, 16, D // 2), bf),
        vm((3, 2, 4, 16, HEAD), f32),
        vm((4, 16, D // 2), bf),
        vm((2, 4, 16, HEAD), f32),
        vm((3, 16, D // 2), bf),
        vm((3, 2, 16, HEAD), f32),
        vm((16, D // 2), bf),
        vm((2, 16, HEAD), f32),
        vm((3, 16, D // 2), bf),
        vm((3, 2, 16, HEAD), f32),
        vm((16, D // 2), bf),
        vm((2, 16, HEAD), f32),
        vm((16, D), bf),
        dma((5,)), dma((8,)), dma((8,)), dma((3, 2, 4)), dma((3, 2, 4)),
        dma((2,)), dma((2,)), dma, dma, dma, dma, dma((4,)), dma((4, CHUNKS, 2)), dma((2,)), dma((7, 4)), dma((7, 4)),
    ]
    video_out, text_out = pl.pallas_call(
        kernel,
        out_shape=(jax.ShapeDtypeStruct((TILE, D), bf), jax.ShapeDtypeStruct((2, D), bf)),
        in_specs=[hbm, hbm, hbm, hbm, pl.BlockSpec(memory_space=pltpu.SMEM)],
        out_specs=(hbm, whole),
        scratch_shapes=scratch,
        compiler_params=pltpu.CompilerParams(
            collective_id=0, has_side_effects=True, vmem_limit_bytes=58 * 2**20
        ),
        cost_estimate=pl.CostEstimate(
            flops=6 * 10**9, bytes_accessed=10**7, transcendentals=12 * 10**6
        ),
    )(video_q[0, 0], video_kv[0, 0], text_qkv, text_mask.reshape(1, 256), pattern.reshape(4))
    return video_out[None, None], text_out


def solution(mesh):
    in_specs = (
        P("ta", "sa", None, None),
        P("ta", "sa", None, None),
        P(("ta", "sa"), None),
        P(),
        P("ta", "sa", None),
    )
    out_specs = (P("ta", "sa", None, None), P(("ta", "sa"), None))
    return jax.shard_map(local, mesh=mesh, in_specs=in_specs, out_specs=out_specs, check_vma=False)
```
